32 devices in a mesh: clu: 32 (over z, y, x, core).
Axes of the slice: x: 2, y: 2, z: 4, core: 2. Of those that a mesh axis runs over, the one named last changes fastest.
Arguments:
- right_sides: float32 [32768, 256], P('clu'), may hold values from -6 to 6
- diag_shift: float32 [32768], P('clu'), may hold values from 1.5 to 3
- near_block: float32 [32768, 1024], P('clu')
- cluster_basis: float32 [32768, 512], P('clu'), may hold values from -0.1875 to 0.1875
- couplings: float32 [192, 512, 512], P('clu'), may hold values from -0.015625 to 0.015625
- partner: int32 [32, 6], P('clu'), may hold values from 1 to 31, as said below
- owned_count: int32 [32], P('clu'), may hold values from 0 to 6, as said below
Outputs:
- solution: float32 [32768, 256], P('clu')
- residual: float32 [32768, 256], P('clu')
The draws below stay inside these ranges and needn't reach their ends.
Inputs may be any that keep to these rules, and one draw needn't show every extreme that they name: `partner`: slots of cluster c below owned_count[c] name distinct clusters c+1 to c+8, ascending; later slots are unused. `owned_count`: cluster 0 owns 6 live slots; the last cluster owns none.
All inputs are finite; a program needn't handle non-finite values.
Results may differ from the reference program's by a relative error of at most 0.0003.
Values sent between devices are 32-bit elements; how exact they have to be, the bound alone decides.
A program may use at most 128 MiB of HBM per device.

```python
import math
import jax
import jax.numpy as jnp
from jax import lax

P_DEV = 1024
K = 512
R = 256
SPAN = 8
SLOTS = 6
ITERS = 2
NPTS = 32768
N_CLU = 32


def pair_table(key):
    scores = jax.random.randint(key, (N_CLU, SPAN), 0, 1 << 20) * SPAN + jnp.arange(SPAN)[None, :]
    chosen = jnp.argsort(scores, axis=1)[:, :SLOTS] + 1
    offsets = jnp.sort(chosen, axis=1)
    anchor = jnp.arange(N_CLU)[:, None]
    reached = anchor + offsets
    partners = jnp.minimum(reached, N_CLU - 1)
    usable = jnp.sum((reached < N_CLU).astype(jnp.int32), axis=1)
    wanted = jax.random.randint(jax.random.fold_in(key, 5), (N_CLU,), 1, SLOTS + 1)
    wanted = jnp.where(jnp.arange(N_CLU) == 0, SLOTS, wanted)
    counts = jnp.minimum(wanted, usable)
    return (partners.astype(jnp.int32), counts.astype(jnp.int32))


def draw_partner(key, part):
    table = pair_table(key)
    return table[0]


def draw_owned_count(key, part):
    table = pair_table(key)
    return table[1]


def draw_near_block(key, part):
    key = jax.random.fold_in(key, 11)
    noise = jax.random.normal(key, (N_CLU, P_DEV, P_DEV), jnp.float32)
    paired = (noise + jnp.transpose(noise, (0, 2, 1))) * (0.07 / P_DEV ** 0.5)
    return paired.reshape(N_CLU * P_DEV, P_DEV).astype(jnp.float32)


def shard_levels(own_key, dims, shards, low, top_value):
    factor_of, own = 1.0, jax.random.fold_in(own_key, 6)
    for axis_at, parts in shards:
        heights = jnp.exp(jax.random.uniform(jax.random.fold_in(own, axis_at), (parts,), jnp.float32, low / len(shards), top_value / len(shards)))
        factor_of = factor_of * jnp.repeat(heights, dims[axis_at] // parts).reshape([-1 if axis == axis_at else 1 for axis in range(len(dims))])
    return factor_of


def normal_values(own_key, shape, spread, bound, pieces=(), dtype=jnp.bfloat16):
    factor_of = shard_levels(own_key, shape, pieces, -0.22, 0.18) if pieces else 1.0
    array = jax.random.normal(own_key, shape, jnp.float32) * spread * factor_of
    return jnp.minimum(jnp.maximum(array, -bound), bound).astype(dtype)


def setup_inputs(seed: int = 0) -> dict:
    streams_of = jax.random.split(jax.random.key(seed), 8)
    right_sides = normal_values(streams_of[0], (NPTS, R), 1.0, 6.0, ((0, 32),), jnp.float32)
    diag_shift = jnp.clip(jnp.exp(math.log(3.0) - 0.6931472 * jax.random.uniform(streams_of[1], (NPTS,), jnp.float32) ** shard_levels(streams_of[1], (NPTS,), ((0, 32),), -0.2, 0.2)), 1.5, 3.0)
    near_block = draw_near_block(jax.random.fold_in(streams_of[7], 71), 0)
    cluster_basis = normal_values(streams_of[3], (NPTS, K), P_DEV ** -0.5, 0.1875, ((0, 32),), jnp.float32)
    couplings = normal_values(streams_of[4], (N_CLU * SLOTS, K, K), (256 * K) ** -0.5, 0.015625, ((0, 32),), jnp.float32)
    partner = draw_partner(jax.random.fold_in(streams_of[7], 71), 0)
    owned_count = draw_owned_count(jax.random.fold_in(streams_of[7], 71), 0)
    return dict(right_sides=right_sides, diag_shift=diag_shift, near_block=near_block, cluster_basis=cluster_basis, couplings=couplings, partner=partner, owned_count=owned_count)


highest = lax.Precision.HIGHEST

def symmetric(matrix):
    return 0.5 * (matrix + matrix.T)

def gram_matrix(left, right):
    return jnp.dot(left.T, right, precision=highest)

def solve_spd(matrix, targets):
    factor = jnp.linalg.cholesky(matrix)
    return jax.scipy.linalg.cho_solve((factor, True), targets)

def apply_operator(vectors, diag_shift, near_block, cluster_basis, couplings, partner, owned_count):
    blocks = vectors.reshape(N_CLU, P_DEV, R)
    nearby = near_block.reshape(N_CLU, P_DEV, P_DEV)
    bases = cluster_basis.reshape(N_CLU, P_DEV, K)
    near_part = jnp.einsum('npq,nqr->npr', nearby, blocks, precision=highest)
    coeffs = jnp.einsum('npk,npr->nkr', bases, blocks, precision=highest)
    live_slots = (jnp.arange(SLOTS)[None, :] < owned_count[:, None]).astype(jnp.float32)
    masked = couplings.reshape(N_CLU, SLOTS, K, K) * live_slots[:, :, None, None]
    partner_coeffs = coeffs[partner]
    far_field = jnp.einsum('nskl,nslr->nkr', masked, partner_coeffs, precision=highest)
    back_terms = jnp.einsum('nskl,nkr->nslr', masked, coeffs, precision=highest)
    far_field = far_field.at[partner.reshape(-1)].add(back_terms.reshape(N_CLU * SLOTS, K, R))
    far_points = jnp.einsum('npk,nkr->npr', bases, far_field, precision=highest)
    return diag_shift[:, None] * vectors + (near_part + far_points).reshape(N_CLU * P_DEV, R)

def reference(right_sides, diag_shift, near_block, cluster_basis, couplings, partner, owned_count):
    solution = jnp.zeros_like(right_sides)
    residual = right_sides
    direction = right_sides
    current = symmetric(gram_matrix(right_sides, right_sides))
    for iteration in range(ITERS):
        image_block = apply_operator(direction, diag_shift, near_block, cluster_basis, couplings, partner, owned_count)
        curvature = symmetric(gram_matrix(direction, image_block))
        alpha_step = solve_spd(curvature, current)
        solution = solution + jnp.dot(direction, alpha_step, precision=highest)
        residual = residual - jnp.dot(image_block, alpha_step, precision=highest)
        if iteration + 1 < ITERS:
            updated = symmetric(gram_matrix(residual, residual))
            beta_step = solve_spd(current, updated)
            direction = residual + jnp.dot(direction, beta_step, precision=highest)
            current = updated
    return (solution, residual)
```

```python
import functools

import jax
import jax.numpy as jnp
from jax import lax
from jax.experimental import pallas as pl
from jax.experimental.pallas import tpu as pltpu
from jax.sharding import PartitionSpec as P

GROUP = 8
MESH = pl.DeviceIdType.MESH
VMEM_LIMIT = 56 * 1024 * 1024

highest = lax.Precision.HIGHEST
high = lax.Precision.HIGH
contract_first = (((0,), (0,)), ((), ()))
contract_last = (((1,), (1,)), ((), ()))
plain = (((1,), (0,)), ((), ()))


def split(x):
    hi = x.astype(jnp.bfloat16)
    return hi, (x - hi.astype(jnp.float32)).astype(jnp.bfloat16)


def dot3(a, b, dims):
    a_hi, a_lo = a
    b_hi, b_lo = b
    d = functools.partial(
        lax.dot_general, dimension_numbers=dims, preferred_element_type=jnp.float32
    )
    return d(a_hi, b_hi) + (d(a_hi, b_lo) + d(a_lo, b_hi))


def far_kernel(n, meta, coef, c_hbm, out, cv, ahead, ret, rs, ri, up, rz,
               c_sem, fs, fr, ss, sr, xs, xr, zs, zr):
    me = lax.axis_index("clu")
    z = me // GROUP
    p = me % GROUP
    a = p // 2
    k = p % 2
    base = z * GROUP
    has_up = z < n // GROUP - 1
    has_down = z > 0
    sib = base + (p + 1 - 2 * k)
    psib = p + 1 - 2 * k
    slots = cv.shape[0]

    def chip(i):
        x, y = a % 2, a // 2
        nx = 1 - x if i & 1 else x
        ny = 1 - y if i & 2 else y
        return ny * 2 + nx

    chips = {i: chip(i) for i in (1, 2, 3)}

    def rc(src, dst, ssem, rsem, dev):
        return pltpu.make_async_remote_copy(
            src_ref=src, dst_ref=dst, send_sem=ssem, recv_sem=rsem,
            device_id=(dev,), device_id_type=MESH)

    c_copy = pltpu.make_async_copy(c_hbm, cv, c_sem)
    c_copy.start()

    @pl.when(jnp.logical_not(has_up))
    def _():
        def zero(j, c):
            ahead[j] = jnp.zeros(ahead.shape[1:], jnp.float32)
            return c
        lax.fori_loop(0, GROUP, zero, 0)

    barrier = pltpu.get_barrier_semaphore()
    pl.semaphore_signal(barrier, inc=1, device_id=(sib,), device_id_type=MESH)
    for i in (1, 2, 3):
        pl.semaphore_signal(barrier, inc=1, device_id=(base + chips[i] * 2 + k,), device_id_type=MESH)

    @pl.when(has_up)
    def _():
        pl.semaphore_signal(barrier, inc=1, device_id=(me + GROUP,), device_id_type=MESH)

    @pl.when(has_down)
    def _():
        pl.semaphore_signal(barrier, inc=1, device_id=(me - GROUP,), device_id_type=MESH)

    pl.semaphore_wait(barrier, 4 + jnp.where(has_up, 1, 0) + jnp.where(has_down, 1, 0))

    f_z = rc(coef, ahead.at[p], fs.at[0], fr.at[0], me - GROUP)

    def f_own(i):
        return rc(coef, ahead.at[p], fs.at[i], fr.at[i], base + chips[i] * 2 + k)

    def f_upper(i):
        return rc(ahead.at[p], ahead.at[p], fs.at[i], fr.at[i], base + chips[i] * 2 + k)

    def f_in(i):
        t = chips[i] * 2 + k
        return rc(ahead.at[t], ahead.at[t], fs.at[3 + i], fr.at[i], sib)

    def f_sib(i):
        t = chips[i] * 2 + k
        return rc(ahead.at[t], ahead.at[t], fs.at[3 + i], fr.at[3 + i], sib)

    def f_sib_in(i):
        t = chips[i] * 2 + 1 - k
        return rc(ahead.at[t], ahead.at[t], fs.at[3 + i], fr.at[3 + i], sib)

    f_s_own = rc(coef, ahead.at[p], fs.at[7], fr.at[7], sib)
    f_s_upper = rc(ahead.at[p], ahead.at[p], fs.at[7], fr.at[7], sib)
    f_s_in = rc(ahead.at[psib], ahead.at[psib], fs.at[7], fr.at[7], sib)

    @pl.when(has_down)
    def _():
        f_z.start()

    for i in (3, 1, 2):
        @pl.when(chips[i] < a)
        def _(i=i):
            f_own(i).start()

    @pl.when(k == 1)
    def _():
        f_s_own.start()

    c_copy.wait()

    def back(t, carry):
        s = meta[0, t]
        term = dot3(split(coef[...]), split(cv[s]), plain)
        ret[t] = jnp.where(meta[1, t] > 0, term, 0.0)
        return carry

    lax.fori_loop(0, GROUP, back, 0)

    r_s = [rc(ret.at[psib], rs.at[0], ss.at[0], sr.at[0], sib)]
    for i in (1, 2, 3):
        r_s.append(rc(ret.at[chips[i] * 2 + 1 - k], rs.at[i], ss.at[i], sr.at[i], sib))
    for i in (3, 1, 2, 0):
        r_s[i].start()

    @pl.when(has_up)
    def _():
        f_z.wait_recv()
        for i in (3, 1, 2):
            @pl.when(chips[i] > a)
            def _(i=i):
                f_upper(i).start()

        @pl.when(k == 0)
        def _():
            f_s_upper.start()

    r_x = [None]
    for i in (1, 2, 3):
        r_x.append(rc(ret.at[chips[i] * 2 + k], ri.at[i - 1], xs.at[i - 1], xr.at[i - 1],
                      base + chips[i] * 2 + k))
    for i in (3, 1, 2):
        r_s[i].wait_recv()
        t = chips[i] * 2 + k
        ret[t] = ret[t] + rs[i]
        r_x[i].start()

    for i in (1, 2, 3):
        @pl.when(jnp.logical_or(chips[i] > a, has_up))
        def _(i=i):
            f_in(i).wait_recv()
            f_sib(i).start()

    r_s[0].wait_recv()
    up[...] = ret[p] + jnp.where(k == 0, rs[0], 0.0)
    out[...] = jnp.where(k == 0, 0.0, rs[0])
    for i in (1, 2, 3):
        r_x[i].wait_recv()
        mine = chips[i] < a
        got = ri[i - 1]
        up[...] += jnp.where(mine, 0.0, got)
        out[...] += jnp.where(mine, got, 0.0)
    r_z = rc(up, rz, zs, zr, me + GROUP)

    @pl.when(has_up)
    def _():
        r_z.start()

    for i in (1, 2, 3):
        @pl.when(jnp.logical_or(chips[i] > a, has_up))
        def _(i=i):
            f_sib_in(i).wait_recv()

    @pl.when(jnp.logical_or(k == 0, has_up))
    def _():
        f_s_in.wait_recv()

    def forth(s, carry):
        block = ahead[meta[2, s]]
        term = dot3(split(block), split(cv[s]), contract_last)
        out[...] += jnp.where(meta[3, s] > 0, term, 0.0)
        return carry

    lax.fori_loop(0, slots, forth, 0)

    @pl.when(has_down)
    def _():
        r_z.wait_recv()
        out[...] += rz[...]
        f_z.wait_send()

    for i in (1, 2, 3):
        @pl.when(jnp.logical_or(chips[i] < a, has_up))
        def _(i=i):
            f_own(i).wait_send()

        @pl.when(jnp.logical_or(chips[i] > a, has_up))
        def _(i=i):
            f_sib(i).wait_send()

        r_x[i].wait_send()
    for i in range(4):
        r_s[i].wait_send()

    @pl.when(jnp.logical_or(k == 1, has_up))
    def _():
        f_s_own.wait_send()

    @pl.when(has_up)
    def _():
        r_z.wait_send()


def far_exchange(n, meta, coef_t, couplings):
    blk = coef_t.shape
    f32 = jnp.float32
    return pl.pallas_call(
        functools.partial(far_kernel, n),
        out_shape=jax.ShapeDtypeStruct(blk, f32),
        in_specs=[
            pl.BlockSpec(memory_space=pltpu.SMEM),
            pl.BlockSpec(memory_space=pltpu.VMEM),
            pl.BlockSpec(memory_space=pl.ANY),
        ],
        out_specs=pl.BlockSpec(memory_space=pltpu.VMEM),
        scratch_shapes=[
            pltpu.VMEM(couplings.shape, f32),
            pltpu.VMEM((GROUP,) + blk, f32),
            pltpu.VMEM((GROUP,) + blk, f32),
            pltpu.VMEM((4,) + blk, f32),
            pltpu.VMEM((3,) + blk, f32),
            pltpu.VMEM(blk, f32),
            pltpu.VMEM(blk, f32),
            pltpu.SemaphoreType.DMA,
            pltpu.SemaphoreType.DMA((8,)),
            pltpu.SemaphoreType.DMA((8,)),
            pltpu.SemaphoreType.DMA((4,)),
            pltpu.SemaphoreType.DMA((4,)),
            pltpu.SemaphoreType.DMA((3,)),
            pltpu.SemaphoreType.DMA((3,)),
            pltpu.SemaphoreType.DMA,
            pltpu.SemaphoreType.DMA,
        ],
        compiler_params=pltpu.CompilerParams(
            collective_id=0, has_side_effects=True, vmem_limit_bytes=VMEM_LIMIT),
        name="far_exchange",
    )(meta, coef_t, couplings)


def sum_kernel(n, g, out, inbox, planes, s1, r1, s2, r2, s3, r3):
    me = lax.axis_index("clu")
    z = me // GROUP
    p = me % GROUP
    base = z * GROUP
    groups = n // GROUP
    rows = g.shape[0] // GROUP

    barrier = pltpu.get_barrier_semaphore()
    for j in range(1, GROUP):
        pl.semaphore_signal(barrier, inc=1, device_id=(base + (p + j) % GROUP,), device_id_type=MESH)
    for j in range(1, groups):
        pl.semaphore_signal(barrier, inc=1, device_id=((me + j * GROUP) % n,), device_id_type=MESH)
    pl.semaphore_wait(barrier, GROUP - 1 + groups - 1)

    def rc(src, dst, ssem, rsem, dev):
        return pltpu.make_async_remote_copy(
            src_ref=src, dst_ref=dst, send_sem=ssem, recv_sem=rsem,
            device_id=(dev,), device_id_type=MESH)

    def part(t):
        return pl.ds(pl.multiple_of(t * rows, 8), rows)

    scatter = []
    for j in range(1, GROUP):
        t = (p + j) % GROUP
        scatter.append(rc(g.at[part(t)], inbox.at[j - 1], s1.at[j - 1], r1.at[j - 1], base + t))
        scatter[-1].start()
    total = g[part(p), :]
    for j in range(1, GROUP):
        scatter[j - 1].wait_recv()
        total = total + inbox[j - 1]
    planes[z] = total
    across = []
    for j in range(1, groups):
        across.append(rc(planes.at[z], planes.at[z], s2.at[j - 1], r2.at[j - 1], (me + j * GROUP) % n))
        across[-1].start()
    for j in range(1, groups):
        src = (z + groups - j) % groups
        rc(planes.at[src], planes.at[src], s2.at[j - 1], r2.at[j - 1], (me + j * GROUP) % n).wait_recv()
    total = planes[0]
    for j in range(1, groups):
        total = total + planes[j]
    out[part(p), :] = total
    gather = []
    for j in range(1, GROUP):
        t = (p + j) % GROUP
        gather.append(rc(out.at[part(p)], out.at[part(p)], s3.at[j - 1], r3.at[j - 1], base + t))
        gather[-1].start()
    for j in range(1, GROUP):
        t = (p + GROUP - j) % GROUP
        rc(out.at[part(t)], out.at[part(t)], s3.at[j - 1], r3.at[j - 1], base + t).wait_recv()
    for copy in scatter + across + gather:
        copy.wait_send()


def sum_all(n, g, collective_id):
    rows = g.shape[0] // GROUP
    groups = n // GROUP
    f32 = jnp.float32
    return pl.pallas_call(
        functools.partial(sum_kernel, n),
        out_shape=jax.ShapeDtypeStruct(g.shape, f32),
        in_specs=[pl.BlockSpec(memory_space=pltpu.VMEM)],
        out_specs=pl.BlockSpec(memory_space=pltpu.VMEM),
        scratch_shapes=[
            pltpu.VMEM((GROUP - 1, rows, g.shape[1]), f32),
            pltpu.VMEM((groups, rows, g.shape[1]), f32),
            pltpu.SemaphoreType.DMA((GROUP - 1,)),
            pltpu.SemaphoreType.DMA((GROUP - 1,)),
            pltpu.SemaphoreType.DMA((groups - 1,)),
            pltpu.SemaphoreType.DMA((groups - 1,)),
            pltpu.SemaphoreType.DMA((GROUP - 1,)),
            pltpu.SemaphoreType.DMA((GROUP - 1,)),
        ],
        compiler_params=pltpu.CompilerParams(
            collective_id=collective_id, has_side_effects=True, vmem_limit_bytes=VMEM_LIMIT),
        name="sum_all_%d" % g.shape[0],
    )(g)


def mm(x, y, dims=plain):
    return lax.dot_general(x, y, dims, precision=highest, preferred_element_type=jnp.float32)


def invert_blocks(mats):
    size = mats[0].shape[0]
    lane = lax.broadcasted_iota(jnp.int32, (1, size), 1)
    sub = lax.broadcasted_iota(jnp.int32, (size, 1), 0)
    mats = list(mats)
    for step in range(size):
        for m, mat in enumerate(mats):
            row = mat[step:step + 1, :]
            col = mat[:, step:step + 1]
            inv = 1.0 / mat[step:step + 1, step:step + 1]
            scaled = jnp.where(lane == step, inv, row * inv)
            factor = jnp.where(sub == step, -1.0, col)
            kept = jnp.where(jnp.logical_or(lane == step, sub == step), 0.0, mat)
            mats[m] = kept - factor * scaled
    return mats


def invert(mats):
    half = mats[0].shape[0] // 2
    a = [m[:half, :half] for m in mats]
    b = [m[:half, half:] for m in mats]
    d = [m[half:, half:] for m in mats]
    ai = invert_blocks(a)
    ab = [mm(x, y) for x, y in zip(ai, b)]
    si = invert_blocks([x - mm(y, w, contract_first) for x, y, w in zip(d, b, ab)])
    result = []
    for x, y, w in zip(ai, ab, si):
        yw = mm(y, w)
        top = jnp.concatenate([x + mm(yw, y, contract_last), -yw], axis=1)
        low = jnp.concatenate([-jnp.transpose(yw), w], axis=1)
        result.append(jnp.concatenate([top, low], axis=0))
    return result


def symmetric(matrix):
    return 0.5 * (matrix + jnp.transpose(matrix))


def first_kernel(grams, alpha_ref, beta_ref):
    size = grams.shape[1]
    g0 = symmetric(grams[:size, :])
    g1 = symmetric(grams[size:2 * size, :])
    g2 = symmetric(grams[2 * size:, :])
    i0, i1 = invert([g0, g1])
    alpha = mm(i1, g0)
    alpha_ref[...] = alpha
    inner = mm(g2, alpha) - g1
    cross = mm(g1, alpha)
    updated = symmetric((g0 - cross) + mm(alpha, inner, contract_first))
    beta_ref[...] = mm(i0, updated)


def second_kernel(curv, cur, alpha_ref):
    (inverse,) = invert([symmetric(curv[...])])
    alpha_ref[...] = mm(inverse, cur[...])


def local_call(kernel, out_shapes, name, *args):
    return pl.pallas_call(
        kernel,
        out_shape=out_shapes,
        compiler_params=pltpu.CompilerParams(vmem_limit_bytes=VMEM_LIMIT),
        name=name,
    )(*args)


def per_device(n, right_sides, diag_shift, near_block, cluster_basis, couplings, partner, owned_count):
    cols = right_sides.shape[1]
    square = jax.ShapeDtypeStruct((cols, cols), jnp.float32)
    slots = partner.shape[1]
    live = jnp.arange(slots) < owned_count[0]
    where_to = partner[0] % GROUP
    match = jnp.logical_and(live[None, :], where_to[None, :] == jnp.arange(GROUP)[:, None])
    pad = [(0, GROUP - slots)]
    meta = jnp.stack([
        jnp.argmax(match, axis=1).astype(jnp.int32),
        jnp.any(match, axis=1).astype(jnp.int32),
        jnp.pad(where_to.astype(jnp.int32), pad),
        jnp.pad(live.astype(jnp.int32), pad),
    ])

    def image_of(vectors):
        coef_t = lax.dot_general(vectors, cluster_basis, contract_first, precision=high)
        near = jnp.dot(near_block, vectors, precision=high)
        far_t = far_exchange(n, meta, coef_t, couplings)
        far = lax.dot_general(cluster_basis, far_t, contract_last, precision=high)
        return diag_shift[:, None] * vectors + (near + far)

    def gram(x, y):
        return lax.dot_general(x, y, contract_first, precision=highest)

    image = image_of(right_sides)
    local = jnp.concatenate([
        gram(right_sides, right_sides), gram(right_sides, image), gram(image, image)])
    grams = sum_all(n, local, 1)
    alpha, beta = local_call(first_kernel, (square, square), "first_steps", grams)
    residual = right_sides - jnp.dot(image, alpha, precision=highest)
    direction = residual + jnp.dot(right_sides, beta, precision=highest)
    image2 = image_of(direction)
    both = jnp.concatenate([gram(direction, image2), gram(residual, residual)])
    summed = sum_all(n, both, 2)
    alpha2 = local_call(second_kernel, square, "second_step", summed[:cols], symmetric(summed[cols:]))
    answer = jnp.dot(right_sides, alpha, precision=highest) + jnp.dot(direction, alpha2, precision=highest)
    residual = residual - jnp.dot(image2, alpha2, precision=highest)
    return answer, residual


def solution(mesh):
    n = mesh.shape["clu"]
    in_specs = (
        P("clu", None),
        P("clu"),
        P("clu", None),
        P("clu", None),
        P("clu", None, None),
        P("clu", None),
        P("clu"),
    )
    out_specs = (P("clu", None), P("clu", None))
    return jax.shard_map(
        functools.partial(per_device, n), mesh=mesh, in_specs=in_specs,
        out_specs=out_specs, check_vma=False)
```

```python
import functools

import jax
import jax.numpy as jnp
from jax import lax
from jax.experimental import pallas as pl
from jax.experimental.pallas import tpu as pltpu
from jax.sharding import PartitionSpec as P

GROUP = 8
MESH = pl.DeviceIdType.MESH
VMEM_LIMIT = 56 * 1024 * 1024

highest = lax.Precision.HIGHEST
high = lax.Precision.HIGH
contract_first = (((0,), (0,)), ((), ()))
contract_last = (((1,), (1,)), ((), ()))
plain = (((1,), (0,)), ((), ()))


def split(x):
    hi = x.astype(jnp.bfloat16)
    return hi, (x - hi.astype(jnp.float32)).astype(jnp.bfloat16)


def dot3(a, b, dims):
    a_hi, a_lo = a
    b_hi, b_lo = b
    d = functools.partial(
        lax.dot_general, dimension_numbers=dims, preferred_element_type=jnp.float32
    )
    return d(a_hi, b_hi) + (d(a_hi, b_lo) + d(a_lo, b_hi))


def far_kernel(n, meta, coef, c_hbm, out, cv, ahead, ret, rs, ri, up, rz,
               c_sem, fs, fr, ss, sr, xs, xr, zs, zr):
    me = lax.axis_index("clu")
    z = me // GROUP
    p = me % GROUP
    a = p // 2
    k = p % 2
    base = z * GROUP
    has_up = z < n // GROUP - 1
    has_down = z > 0
    sib = base + (p + 1 - 2 * k)
    psib = p + 1 - 2 * k
    slots = cv.shape[0]

    def chip(i):
        x, y = a % 2, a // 2
        nx = 1 - x if i & 1 else x
        ny = 1 - y if i & 2 else y
        return ny * 2 + nx

    chips = {i: chip(i) for i in (1, 2, 3)}

    def rc(src, dst, ssem, rsem, dev):
        return pltpu.make_async_remote_copy(
            src_ref=src, dst_ref=dst, send_sem=ssem, recv_sem=rsem,
            device_id=(dev,), device_id_type=MESH)

    c_copy = pltpu.make_async_copy(c_hbm, cv, c_sem)
    c_copy.start()

    @pl.when(jnp.logical_not(has_up))
    def _():
        def zero(j, c):
            ahead[j] = jnp.zeros(ahead.shape[1:], jnp.float32)
            return c
        lax.fori_loop(0, GROUP, zero, 0)

    barrier = pltpu.get_barrier_semaphore()
    pl.semaphore_signal(barrier, inc=1, device_id=(sib,), device_id_type=MESH)
    for i in (1, 2, 3):
        pl.semaphore_signal(barrier, inc=1, device_id=(base + chips[i] * 2 + k,), device_id_type=MESH)

    @pl.when(has_up)
    def _():
        pl.semaphore_signal(barrier, inc=1, device_id=(me + GROUP,), device_id_type=MESH)

    @pl.when(has_down)
    def _():
        pl.semaphore_signal(barrier, inc=1, device_id=(me - GROUP,), device_id_type=MESH)

    pl.semaphore_wait(barrier, 4 + jnp.where(has_up, 1, 0) + jnp.where(has_down, 1, 0))

    f_z = rc(coef, ahead.at[p], fs.at[0], fr.at[0], me - GROUP)

    def f_own(i):
        return rc(coef, ahead.at[p], fs.at[i], fr.at[i], base + chips[i] * 2 + k)

    def f_upper(i):
        return rc(ahead.at[p], ahead.at[p], fs.at[i], fr.at[i], base + chips[i] * 2 + k)

    def f_in(i):
        t = chips[i] * 2 + k
        return rc(ahead.at[t], ahead.at[t], fs.at[3 + i], fr.at[i], sib)

    def f_sib(i):
        t = chips[i] * 2 + k
        return rc(ahead.at[t], ahead.at[t], fs.at[3 + i], fr.at[3 + i], sib)

    def f_sib_in(i):
        t = chips[i] * 2 + 1 - k
        return rc(ahead.at[t], ahead.at[t], fs.at[3 + i], fr.at[3 + i], sib)

    f_s_own = rc(coef, ahead.at[p], fs.at[7], fr.at[7], sib)
    f_s_upper = rc(ahead.at[p], ahead.at[p], fs.at[7], fr.at[7], sib)
    f_s_in = rc(ahead.at[psib], ahead.at[psib], fs.at[7], fr.at[7], sib)

    @pl.when(has_down)
    def _():
        f_z.start()

    for i in (3, 1, 2):
        @pl.when(chips[i] < a)
        def _(i=i):
            f_own(i).start()

    @pl.when(k == 1)
    def _():
        f_s_own.start()

    c_copy.wait()

    def back(t, carry):
        s = meta[0, t]
        term = dot3(split(coef[...]), split(cv[s]), plain)
        ret[t] = jnp.where(meta[1, t] > 0, term, 0.0)
        return carry

    lax.fori_loop(0, GROUP, back, 0)

    r_s = [rc(ret.at[psib], rs.at[0], ss.at[0], sr.at[0], sib)]
    for i in (1, 2, 3):
        r_s.append(rc(ret.at[chips[i] * 2 + 1 - k], rs.at[i], ss.at[i], sr.at[i], sib))
    for i in (3, 1, 2, 0):
        r_s[i].start()

    @pl.when(has_up)
    def _():
        f_z.wait_recv()
        for i in (3, 1, 2):
            @pl.when(chips[i] > a)
            def _(i=i):
                f_upper(i).start()

        @pl.when(k == 0)
        def _():
            f_s_upper.start()

    r_x = [None]
    for i in (1, 2, 3):
        r_x.append(rc(ret.at[chips[i] * 2 + k], ri.at[i - 1], xs.at[i - 1], xr.at[i - 1],
                      base + chips[i] * 2 + k))
    for i in (3, 1, 2):
        r_s[i].wait_recv()
        t = chips[i] * 2 + k
        ret[t] = ret[t] + rs[i]
        r_x[i].start()

    for i in (1, 2, 3):
        @pl.when(jnp.logical_or(chips[i] > a, has_up))
        def _(i=i):
            f_in(i).wait_recv()
            f_sib(i).start()

    r_s[0].wait_recv()
    up[...] = ret[p] + jnp.where(k == 0, rs[0], 0.0)
    out[...] = jnp.where(k == 0, 0.0, rs[0])
    for i in (1, 2, 3):
        r_x[i].wait_recv()
        mine = chips[i] < a
        got = ri[i - 1]
        up[...] += jnp.where(mine, 0.0, got)
        out[...] += jnp.where(mine, got, 0.0)
    r_z = rc(up, rz, zs, zr, me + GROUP)

    @pl.when(has_up)
    def _():
        r_z.start()

    for i in (1, 2, 3):
        @pl.when(jnp.logical_or(chips[i] > a, has_up))
        def _(i=i):
            f_sib_in(i).wait_recv()

    @pl.when(jnp.logical_or(k == 0, has_up))
    def _():
        f_s_in.wait_recv()

    def forth(s, carry):
        block = ahead[meta[2, s]]
        term = dot3(split(block), split(cv[s]), contract_last)
        out[...] += jnp.where(meta[3, s] > 0, term, 0.0)
        return carry

    lax.fori_loop(0, slots, forth, 0)

    @pl.when(has_down)
    def _():
        r_z.wait_recv()
        out[...] += rz[...]
        f_z.wait_send()

    for i in (1, 2, 3):
        @pl.when(jnp.logical_or(chips[i] < a, has_up))
        def _(i=i):
            f_own(i).wait_send()

        @pl.when(jnp.logical_or(chips[i] > a, has_up))
        def _(i=i):
            f_sib(i).wait_send()

        r_x[i].wait_send()
    for i in range(4):
        r_s[i].wait_send()

    @pl.when(jnp.logical_or(k == 1, has_up))
    def _():
        f_s_own.wait_send()

    @pl.when(has_up)
    def _():
        r_z.wait_send()


def far_exchange(n, meta, coef_t, couplings):
    blk = coef_t.shape
    f32 = jnp.float32
    return pl.pallas_call(
        functools.partial(far_kernel, n),
        out_shape=jax.ShapeDtypeStruct(blk, f32),
        in_specs=[
            pl.BlockSpec(memory_space=pltpu.SMEM),
            pl.BlockSpec(memory_space=pltpu.VMEM),
            pl.BlockSpec(memory_space=pl.ANY),
        ],
        out_specs=pl.BlockSpec(memory_space=pltpu.VMEM),
        scratch_shapes=[
            pltpu.VMEM(couplings.shape, f32),
            pltpu.VMEM((GROUP,) + blk, f32),
            pltpu.VMEM((GROUP,) + blk, f32),
            pltpu.VMEM((4,) + blk, f32),
            pltpu.VMEM((3,) + blk, f32),
            pltpu.VMEM(blk, f32),
            pltpu.VMEM(blk, f32),
            pltpu.SemaphoreType.DMA,
            pltpu.SemaphoreType.DMA((8,)),
            pltpu.SemaphoreType.DMA((8,)),
            pltpu.SemaphoreType.DMA((4,)),
            pltpu.SemaphoreType.DMA((4,)),
            pltpu.SemaphoreType.DMA((3,)),
            pltpu.SemaphoreType.DMA((3,)),
            pltpu.SemaphoreType.DMA,
            pltpu.SemaphoreType.DMA,
        ],
        compiler_params=pltpu.CompilerParams(
            collective_id=0, has_side_effects=True, vmem_limit_bytes=VMEM_LIMIT),
        name="far_exchange",
    )(meta, coef_t, couplings)


def sum_kernel(n, g, out, inbox, planes, s1, r1, s2, r2, s3, r3):
    me = lax.axis_index("clu")
    z = me // GROUP
    p = me % GROUP
    base = z * GROUP
    groups = n // GROUP
    rows = g.shape[0] // GROUP

    barrier = pltpu.get_barrier_semaphore()
    for j in range(1, GROUP):
        pl.semaphore_signal(barrier, inc=1, device_id=(base + (p + j) % GROUP,), device_id_type=MESH)
    for j in range(1, groups):
        pl.semaphore_signal(barrier, inc=1, device_id=((me + j * GROUP) % n,), device_id_type=MESH)
    pl.semaphore_wait(barrier, GROUP - 1 + groups - 1)

    def rc(src, dst, ssem, rsem, dev):
        return pltpu.make_async_remote_copy(
            src_ref=src, dst_ref=dst, send_sem=ssem, recv_sem=rsem,
            device_id=(dev,), device_id_type=MESH)

    def part(t):
        return pl.ds(pl.multiple_of(t * rows, 8), rows)

    scatter = []
    for j in range(1, GROUP):
        t = (p + j) % GROUP
        scatter.append(rc(g.at[part(t)], inbox.at[j - 1], s1.at[j - 1], r1.at[j - 1], base + t))
        scatter[-1].start()
    total = g[part(p), :]
    for j in range(1, GROUP):
        scatter[j - 1].wait_recv()
        total = total + inbox[j - 1]
    planes[z] = total
    across = []
    for j in range(1, groups):
        across.append(rc(planes.at[z], planes.at[z], s2.at[j - 1], r2.at[j - 1], (me + j * GROUP) % n))
        across[-1].start()
    for j in range(1, groups):
        src = (z + groups - j) % groups
        rc(planes.at[src], planes.at[src], s2.at[j - 1], r2.at[j - 1], (me + j * GROUP) % n).wait_recv()
    total = planes[0]
    for j in range(1, groups):
        total = total + planes[j]
    out[part(p), :] = total
    gather = []
    for j in range(1, GROUP):
        t = (p + j) % GROUP
        gather.append(rc(out.at[part(p)], out.at[part(p)], s3.at[j - 1], r3.at[j - 1], base + t))
        gather[-1].start()
    for j in range(1, GROUP):
        t = (p + GROUP - j) % GROUP
        rc(out.at[part(t)], out.at[part(t)], s3.at[j - 1], r3.at[j - 1], base + t).wait_recv()
    for copy in scatter + across + gather:
        copy.wait_send()


def sum_all(n, g, collective_id):
    rows = g.shape[0] // GROUP
    groups = n // GROUP
    f32 = jnp.float32
    return pl.pallas_call(
        functools.partial(sum_kernel, n),
        out_shape=jax.ShapeDtypeStruct(g.shape, f32),
        in_specs=[pl.BlockSpec(memory_space=pltpu.VMEM)],
        out_specs=pl.BlockSpec(memory_space=pltpu.VMEM),
        scratch_shapes=[
            pltpu.VMEM((GROUP - 1, rows, g.shape[1]), f32),
            pltpu.VMEM((groups, rows, g.shape[1]), f32),
            pltpu.SemaphoreType.DMA((GROUP - 1,)),
            pltpu.SemaphoreType.DMA((GROUP - 1,)),
            pltpu.SemaphoreType.DMA((groups - 1,)),
            pltpu.SemaphoreType.DMA((groups - 1,)),
            pltpu.SemaphoreType.DMA((GROUP - 1,)),
            pltpu.SemaphoreType.DMA((GROUP - 1,)),
        ],
        compiler_params=pltpu.CompilerParams(
            collective_id=collective_id, has_side_effects=True, vmem_limit_bytes=VMEM_LIMIT),
        name="sum_all_%d" % g.shape[0],
    )(g)


def mm(x, y, dims=plain):
    return lax.dot_general(x, y, dims, precision=highest, preferred_element_type=jnp.float32)


def invert_blocks(mats):
    size = mats[0].shape[0]
    lane = lax.broadcasted_iota(jnp.int32, (1, size), 1)
    sub = lax.broadcasted_iota(jnp.int32, (size, 1), 0)
    mats = list(mats)
    for k0 in range(0, size, 2):
        k1 = k0 + 1
        at_lane = jnp.logical_or(lane == k0, lane == k1)
        at_sub = jnp.logical_or(sub == k0, sub == k1)
        for m, mat in enumerate(mats):
            row0, row1 = mat[k0:k1, :], mat[k1:k1 + 1, :]
            col0, col1 = mat[:, k0:k1], mat[:, k1:k1 + 1]
            p00, p01 = row0[:, k0:k1], row0[:, k1:k1 + 1]
            p10, p11 = row1[:, k0:k1], row1[:, k1:k1 + 1]
            inv = 1.0 / (p00 * p11 - p01 * p10)
            unit0 = jnp.where(lane == k0, 1.0, jnp.where(lane == k1, 0.0, row0))
            unit1 = jnp.where(lane == k1, 1.0, jnp.where(lane == k0, 0.0, row1))
            scaled0 = (p11 * unit0 - p01 * unit1) * inv
            scaled1 = (p00 * unit1 - p10 * unit0) * inv
            factor0 = jnp.where(sub == k0, -1.0, jnp.where(sub == k1, 0.0, col0))
            factor1 = jnp.where(sub == k1, -1.0, jnp.where(sub == k0, 0.0, col1))
            kept = jnp.where(jnp.logical_or(at_lane, at_sub), 0.0, mat)
            mats[m] = (kept - factor0 * scaled0) - factor1 * scaled1
    return mats


def invert(mats):
    half = mats[0].shape[0] // 2
    a = [m[:half, :half] for m in mats]
    b = [m[:half, half:] for m in mats]
    d = [m[half:, half:] for m in mats]
    ai = invert_blocks(a)
    ab = [mm(x, y) for x, y in zip(ai, b)]
    si = invert_blocks([x - mm(y, w, contract_first) for x, y, w in zip(d, b, ab)])
    result = []
    for x, y, w in zip(ai, ab, si):
        yw = mm(y, w)
        top = jnp.concatenate([x + mm(yw, y, contract_last), -yw], axis=1)
        low = jnp.concatenate([-jnp.transpose(yw), w], axis=1)
        result.append(jnp.concatenate([top, low], axis=0))
    return result


def symmetric(matrix):
    return 0.5 * (matrix + jnp.transpose(matrix))


def first_kernel(grams, alpha_ref, beta_ref, updated_ref):
    size = grams.shape[1]
    g0 = symmetric(grams[:size, :])
    g1 = symmetric(grams[size:2 * size, :])
    g2 = symmetric(grams[2 * size:, :])
    i0, i1 = invert([g0, g1])
    alpha = mm(i1, g0)
    alpha_ref[...] = alpha
    inner = mm(g2, alpha) - g1
    cross = mm(g1, alpha)
    updated = symmetric((g0 - cross) + mm(alpha, inner, contract_first))
    updated_ref[...] = updated
    beta_ref[...] = mm(i0, updated)


def second_kernel(curv, cur, alpha_ref):
    (inverse,) = invert([symmetric(curv[...])])
    alpha_ref[...] = mm(inverse, cur[...])


def local_call(kernel, out_shapes, name, *args):
    return pl.pallas_call(
        kernel,
        out_shape=out_shapes,
        compiler_params=pltpu.CompilerParams(vmem_limit_bytes=VMEM_LIMIT),
        name=name,
    )(*args)


def per_device(n, right_sides, diag_shift, near_block, cluster_basis, couplings, partner, owned_count):
    cols = right_sides.shape[1]
    square = jax.ShapeDtypeStruct((cols, cols), jnp.float32)
    slots = partner.shape[1]
    live = jnp.arange(slots) < owned_count[0]
    where_to = partner[0] % GROUP
    match = jnp.logical_and(live[None, :], where_to[None, :] == jnp.arange(GROUP)[:, None])
    pad = [(0, GROUP - slots)]
    meta = jnp.stack([
        jnp.argmax(match, axis=1).astype(jnp.int32),
        jnp.any(match, axis=1).astype(jnp.int32),
        jnp.pad(where_to.astype(jnp.int32), pad),
        jnp.pad(live.astype(jnp.int32), pad),
    ])

    def image_of(vectors):
        coef_t = lax.dot_general(vectors, cluster_basis, contract_first, precision=high)
        near = jnp.dot(near_block, vectors, precision=high)
        far_t = far_exchange(n, meta, coef_t, couplings)
        far = lax.dot_general(cluster_basis, far_t, contract_last, precision=high)
        return diag_shift[:, None] * vectors + (near + far)

    def gram(x, y):
        return lax.dot_general(x, y, contract_first, precision=highest)

    image = image_of(right_sides)
    local = jnp.concatenate([
        gram(right_sides, right_sides), gram(right_sides, image), gram(image, image)])
    grams = sum_all(n, local, 1)
    alpha, beta, updated = local_call(first_kernel, (square,) * 3, "first_steps", grams)
    residual = right_sides - jnp.dot(image, alpha, precision=highest)
    direction = residual + jnp.dot(right_sides, beta, precision=highest)
    image2 = image_of(direction)
    curvature = sum_all(n, gram(direction, image2), 2)
    alpha2 = local_call(second_kernel, square, "second_step", curvature, updated)
    answer = jnp.dot(right_sides, alpha, precision=highest) + jnp.dot(direction, alpha2, precision=highest)
    residual = residual - jnp.dot(image2, alpha2, precision=highest)
    return answer, residual


def solution(mesh):
    n = mesh.shape["clu"]
    in_specs = (
        P("clu", None),
        P("clu"),
        P("clu", None),
        P("clu", None),
        P("clu", None, None),
        P("clu", None),
        P("clu"),
    )
    out_specs = (P("clu", None), P("clu", None))
    return jax.shard_map(
        functools.partial(per_device, n), mesh=mesh, in_specs=in_specs,
        out_specs=out_specs, check_vma=False)
```

```python
import functools

import jax
import jax.numpy as jnp
from jax import lax
from jax.experimental import pallas as pl
from jax.experimental.pallas import tpu as pltpu
from jax.sharding import PartitionSpec as P

GROUP = 8
MESH = pl.DeviceIdType.MESH
VMEM_LIMIT = 56 * 1024 * 1024

highest = lax.Precision.HIGHEST
high = lax.Precision.HIGH
contract_first = (((0,), (0,)), ((), ()))
contract_last = (((1,), (1,)), ((), ()))
plain = (((1,), (0,)), ((), ()))


def split(x):
    hi = x.astype(jnp.bfloat16)
    return hi, (x - hi.astype(jnp.float32)).astype(jnp.bfloat16)


def dot3(a, b, dims):
    a_hi, a_lo = a
    b_hi, b_lo = b
    d = functools.partial(
        lax.dot_general, dimension_numbers=dims, preferred_element_type=jnp.float32
    )
    return d(a_hi, b_hi) + (d(a_hi, b_lo) + d(a_lo, b_hi))


def far_kernel(n, solve, *refs):
    if solve:
        meta, coef, c_hbm, grams, out, alpha, beta, updated = refs[:8]
        refs = refs[8:]
    else:
        meta, coef, c_hbm, out = refs[:4]
        refs = refs[4:]
    cv, ahead, ret, rs, ri, up, rz, c_sem, fs, fr, ss, sr, xs, xr, zs, zr = refs[:16]
    me = lax.axis_index("clu")
    z = me // GROUP
    p = me % GROUP
    a = p // 2
    k = p % 2
    base = z * GROUP
    has_up = z < n // GROUP - 1
    has_down = z > 0
    sib = base + (p + 1 - 2 * k)
    psib = p + 1 - 2 * k
    slots = cv.shape[0]

    def chip(i):
        x, y = a % 2, a // 2
        nx = 1 - x if i & 1 else x
        ny = 1 - y if i & 2 else y
        return ny * 2 + nx

    chips = {i: chip(i) for i in (1, 2, 3)}

    def rc(src, dst, ssem, rsem, dev):
        return pltpu.make_async_remote_copy(
            src_ref=src, dst_ref=dst, send_sem=ssem, recv_sem=rsem,
            device_id=(dev,), device_id_type=MESH)

    c_copy = pltpu.make_async_copy(c_hbm, cv, c_sem)
    c_copy.start()

    @pl.when(jnp.logical_not(has_up))
    def _():
        def zero(j, c):
            ahead[j] = jnp.zeros(ahead.shape[1:], jnp.float32)
            return c
        lax.fori_loop(0, GROUP, zero, 0)

    if solve:
        greet_all(n, me)
    else:
        barrier = pltpu.get_barrier_semaphore()
        pl.semaphore_signal(barrier, inc=1, device_id=(sib,), device_id_type=MESH)
        for i in (1, 2, 3):
            pl.semaphore_signal(barrier, inc=1, device_id=(base + chips[i] * 2 + k,), device_id_type=MESH)

        @pl.when(has_up)
        def _():
            pl.semaphore_signal(barrier, inc=1, device_id=(me + GROUP,), device_id_type=MESH)

        @pl.when(has_down)
        def _():
            pl.semaphore_signal(barrier, inc=1, device_id=(me - GROUP,), device_id_type=MESH)

        pl.semaphore_wait(barrier, 4 + jnp.where(has_up, 1, 0) + jnp.where(has_down, 1, 0))

    f_z = rc(coef, ahead.at[p], fs.at[0], fr.at[0], me - GROUP)

    def f_own(i):
        return rc(coef, ahead.at[p], fs.at[i], fr.at[i], base + chips[i] * 2 + k)

    def f_upper(i):
        return rc(ahead.at[p], ahead.at[p], fs.at[i], fr.at[i], base + chips[i] * 2 + k)

    def f_in(i):
        t = chips[i] * 2 + k
        return rc(ahead.at[t], ahead.at[t], fs.at[3 + i], fr.at[i], sib)

    def f_sib(i):
        t = chips[i] * 2 + k
        return rc(ahead.at[t], ahead.at[t], fs.at[3 + i], fr.at[3 + i], sib)

    def f_sib_in(i):
        t = chips[i] * 2 + 1 - k
        return rc(ahead.at[t], ahead.at[t], fs.at[3 + i], fr.at[3 + i], sib)

    f_s_own = rc(coef, ahead.at[p], fs.at[7], fr.at[7], sib)
    f_s_upper = rc(ahead.at[p], ahead.at[p], fs.at[7], fr.at[7], sib)
    f_s_in = rc(ahead.at[psib], ahead.at[psib], fs.at[7], fr.at[7], sib)

    @pl.when(has_down)
    def _():
        f_z.start()

    for i in (3, 1, 2):
        @pl.when(chips[i] < a)
        def _(i=i):
            f_own(i).start()

    @pl.when(k == 1)
    def _():
        f_s_own.start()

    if solve:
        total = refs[16]
        finish_sum, drain_sum = start_sum(n, me, grams, total, *refs[17:])

    c_copy.wait()

    def back(t, carry):
        s = meta[0, t]
        term = dot3(split(coef[...]), split(cv[s]), plain)
        ret[t] = jnp.where(meta[1, t] > 0, term, 0.0)
        return carry

    lax.fori_loop(0, GROUP, back, 0)

    r_s = [rc(ret.at[psib], rs.at[0], ss.at[0], sr.at[0], sib)]
    for i in (1, 2, 3):
        r_s.append(rc(ret.at[chips[i] * 2 + 1 - k], rs.at[i], ss.at[i], sr.at[i], sib))
    for i in (3, 1, 2, 0):
        r_s[i].start()

    @pl.when(has_up)
    def _():
        f_z.wait_recv()
        for i in (3, 1, 2):
            @pl.when(chips[i] > a)
            def _(i=i):
                f_upper(i).start()

        @pl.when(k == 0)
        def _():
            f_s_upper.start()

    r_x = [None]
    for i in (1, 2, 3):
        r_x.append(rc(ret.at[chips[i] * 2 + k], ri.at[i - 1], xs.at[i - 1], xr.at[i - 1],
                      base + chips[i] * 2 + k))
    for i in (3, 1, 2):
        r_s[i].wait_recv()
        t = chips[i] * 2 + k
        ret[t] = ret[t] + rs[i]
        r_x[i].start()

    if solve:
        finish_sum()
        first_kernel(total, alpha, beta, updated)

    for i in (1, 2, 3):
        @pl.when(jnp.logical_or(chips[i] > a, has_up))
        def _(i=i):
            f_in(i).wait_recv()
            f_sib(i).start()

    r_s[0].wait_recv()
    up[...] = ret[p] + jnp.where(k == 0, rs[0], 0.0)
    out[...] = jnp.where(k == 0, 0.0, rs[0])
    for i in (1, 2, 3):
        r_x[i].wait_recv()
        mine = chips[i] < a
        got = ri[i - 1]
        up[...] += jnp.where(mine, 0.0, got)
        out[...] += jnp.where(mine, got, 0.0)
    r_z = rc(up, rz, zs, zr, me + GROUP)

    @pl.when(has_up)
    def _():
        r_z.start()

    for i in (1, 2, 3):
        @pl.when(jnp.logical_or(chips[i] > a, has_up))
        def _(i=i):
            f_sib_in(i).wait_recv()

    @pl.when(jnp.logical_or(k == 0, has_up))
    def _():
        f_s_in.wait_recv()

    def forth(s, carry):
        block = ahead[meta[2, s]]
        term = dot3(split(block), split(cv[s]), contract_last)
        out[...] += jnp.where(meta[3, s] > 0, term, 0.0)
        return carry

    lax.fori_loop(0, slots, forth, 0)

    @pl.when(has_down)
    def _():
        r_z.wait_recv()
        out[...] += rz[...]
        f_z.wait_send()

    for i in (1, 2, 3):
        @pl.when(jnp.logical_or(chips[i] < a, has_up))
        def _(i=i):
            f_own(i).wait_send()

        @pl.when(jnp.logical_or(chips[i] > a, has_up))
        def _(i=i):
            f_sib(i).wait_send()

        r_x[i].wait_send()
    for i in range(4):
        r_s[i].wait_send()

    @pl.when(jnp.logical_or(k == 1, has_up))
    def _():
        f_s_own.wait_send()

    @pl.when(has_up)
    def _():
        r_z.wait_send()

    if solve:
        drain_sum()


def far_exchange(n, meta, coef_t, couplings, grams=None):
    blk = coef_t.shape
    f32 = jnp.float32
    solve = grams is not None
    vmem = pl.BlockSpec(memory_space=pltpu.VMEM)
    one = jax.ShapeDtypeStruct(blk, f32)
    extra = []
    if solve:
        square = jax.ShapeDtypeStruct((grams.shape[1],) * 2, f32)
        extra = [pltpu.VMEM(grams.shape, f32)] + sum_scratch(n, grams)
    return pl.pallas_call(
        functools.partial(far_kernel, n, solve),
        out_shape=(one, square, square, square) if solve else one,
        in_specs=[
            pl.BlockSpec(memory_space=pltpu.SMEM),
            pl.BlockSpec(memory_space=pltpu.VMEM),
            pl.BlockSpec(memory_space=pl.ANY),
        ] + [vmem] * solve,
        out_specs=(vmem,) * 4 if solve else vmem,
        scratch_shapes=[
            pltpu.VMEM(couplings.shape, f32),
            pltpu.VMEM((GROUP,) + blk, f32),
            pltpu.VMEM((GROUP,) + blk, f32),
            pltpu.VMEM((4,) + blk, f32),
            pltpu.VMEM((3,) + blk, f32),
            pltpu.VMEM(blk, f32),
            pltpu.VMEM(blk, f32),
            pltpu.SemaphoreType.DMA,
            pltpu.SemaphoreType.DMA((8,)),
            pltpu.SemaphoreType.DMA((8,)),
            pltpu.SemaphoreType.DMA((4,)),
            pltpu.SemaphoreType.DMA((4,)),
            pltpu.SemaphoreType.DMA((3,)),
            pltpu.SemaphoreType.DMA((3,)),
            pltpu.SemaphoreType.DMA,
            pltpu.SemaphoreType.DMA,
        ] + extra,
        compiler_params=pltpu.CompilerParams(
            collective_id=int(solve), has_side_effects=True, vmem_limit_bytes=VMEM_LIMIT),
        name="far_exchange_solve" if solve else "far_exchange",
    )(meta, coef_t, couplings, *([grams] if solve else []))


def greet_all(n, me):
    base, p, groups = me // GROUP * GROUP, me % GROUP, n // GROUP
    barrier = pltpu.get_barrier_semaphore()
    for j in range(1, GROUP):
        pl.semaphore_signal(barrier, inc=1, device_id=(base + (p + j) % GROUP,), device_id_type=MESH)
    for j in range(1, groups):
        pl.semaphore_signal(barrier, inc=1, device_id=((me + j * GROUP) % n,), device_id_type=MESH)
    pl.semaphore_wait(barrier, GROUP - 1 + groups - 1)


def start_sum(n, me, g, out, inbox, planes, s1, r1, s2, r2, s3, r3):
    z = me // GROUP
    p = me % GROUP
    base = z * GROUP
    groups = n // GROUP
    rows = g.shape[0] // GROUP
    pending = []

    def rc(src, dst, ssem, rsem, dev):
        return pltpu.make_async_remote_copy(
            src_ref=src, dst_ref=dst, send_sem=ssem, recv_sem=rsem,
            device_id=(dev,), device_id_type=MESH)

    def part(t):
        return pl.ds(pl.multiple_of(t * rows, 8), rows)

    for j in range(1, GROUP):
        t = (p + j) % GROUP
        pending.append(rc(g.at[part(t)], inbox.at[j - 1], s1.at[j - 1], r1.at[j - 1], base + t))
        pending[-1].start()
    scatter = list(pending)

    def finish():
        total = g[part(p), :]
        for j in range(1, GROUP):
            scatter[j - 1].wait_recv()
            total = total + inbox[j - 1]
        planes[z] = total
        for j in range(1, groups):
            pending.append(rc(planes.at[z], planes.at[z], s2.at[j - 1], r2.at[j - 1], (me + j * GROUP) % n))
            pending[-1].start()
        for j in range(1, groups):
            src = (z + groups - j) % groups
            rc(planes.at[src], planes.at[src], s2.at[j - 1], r2.at[j - 1], (me + j * GROUP) % n).wait_recv()
        total = planes[0]
        for j in range(1, groups):
            total = total + planes[j]
        out[part(p), :] = total
        for j in range(1, GROUP):
            t = (p + j) % GROUP
            pending.append(rc(out.at[part(p)], out.at[part(p)], s3.at[j - 1], r3.at[j - 1], base + t))
            pending[-1].start()
        for j in range(1, GROUP):
            t = (p + GROUP - j) % GROUP
            rc(out.at[part(t)], out.at[part(t)], s3.at[j - 1], r3.at[j - 1], base + t).wait_recv()

    def drain():
        for copy in pending:
            copy.wait_send()

    return finish, drain


def sum_kernel(n, g, out, *refs):
    me = lax.axis_index("clu")
    greet_all(n, me)
    finish, drain = start_sum(n, me, g, out, *refs)
    finish()
    drain()


def sum_scratch(n, g):
    rows, groups = g.shape[0] // GROUP, n // GROUP
    counts = (GROUP - 1, GROUP - 1, groups - 1, groups - 1, GROUP - 1, GROUP - 1)
    return [
        pltpu.VMEM((GROUP - 1, rows, g.shape[1]), jnp.float32),
        pltpu.VMEM((groups, rows, g.shape[1]), jnp.float32),
    ] + [pltpu.SemaphoreType.DMA((c,)) for c in counts]


def sum_all(n, g, collective_id):
    f32 = jnp.float32
    return pl.pallas_call(
        functools.partial(sum_kernel, n),
        out_shape=jax.ShapeDtypeStruct(g.shape, f32),
        in_specs=[pl.BlockSpec(memory_space=pltpu.VMEM)],
        out_specs=pl.BlockSpec(memory_space=pltpu.VMEM),
        scratch_shapes=sum_scratch(n, g),
        compiler_params=pltpu.CompilerParams(
            collective_id=collective_id, has_side_effects=True, vmem_limit_bytes=VMEM_LIMIT),
        name="sum_all_%d" % g.shape[0],
    )(g)


def mm(x, y, dims=plain):
    return lax.dot_general(x, y, dims, precision=highest, preferred_element_type=jnp.float32)


def invert_blocks(mats):
    size = mats[0].shape[0]
    lane = lax.broadcasted_iota(jnp.int32, (1, size), 1)
    sub = lax.broadcasted_iota(jnp.int32, (size, 1), 0)
    unroll = 8

    def body(_, state):
        state = list(state)
        for step in range(unroll):
            for m, mat in enumerate(state):
                row = mat[step:step + 1, :]
                col = mat[:, step:step + 1]
                inv = 1.0 / mat[step:step + 1, step:step + 1]
                scaled = jnp.where(lane == step, inv, row * inv)
                factor = jnp.where(sub == step, -1.0, col)
                kept = jnp.where(jnp.logical_or(lane == step, sub == step), 0.0, mat)
                state[m] = kept - factor * scaled
        state = [jnp.concatenate([x[unroll:], x[:unroll]], axis=0) for x in state]
        return tuple(pltpu.roll(x, size - unroll, 1) for x in state)

    return list(lax.fori_loop(0, size // unroll, body, tuple(mats)))


def invert(mats):
    half = mats[0].shape[0] // 2
    a = [m[:half, :half] for m in mats]
    b = [m[:half, half:] for m in mats]
    d = [m[half:, half:] for m in mats]
    ai = invert_blocks(a)
    ab = [mm(x, y) for x, y in zip(ai, b)]
    si = invert_blocks([x - mm(y, w, contract_first) for x, y, w in zip(d, b, ab)])
    result = []
    for x, y, w in zip(ai, ab, si):
        yw = mm(y, w)
        top = jnp.concatenate([x + mm(yw, y, contract_last), -yw], axis=1)
        low = jnp.concatenate([-jnp.transpose(yw), w], axis=1)
        result.append(jnp.concatenate([top, low], axis=0))
    return result


def symmetric(matrix):
    return 0.5 * (matrix + jnp.transpose(matrix))


def first_kernel(grams, alpha_ref, beta_ref, updated_ref):
    size = grams.shape[1]
    g0 = symmetric(grams[:size, :])
    g1 = symmetric(grams[size:2 * size, :])
    g2 = symmetric(grams[2 * size:, :])
    i0, i1 = invert([g0, g1])
    alpha = mm(i1, g0)
    alpha_ref[...] = alpha
    inner = mm(g2, alpha) - g1
    cross = mm(g1, alpha)
    updated = symmetric((g0 - cross) + mm(alpha, inner, contract_first))
    updated_ref[...] = updated
    beta_ref[...] = mm(i0, updated)


def second_kernel(curv, cur, alpha_ref):
    (inverse,) = invert([symmetric(curv[...])])
    alpha_ref[...] = mm(inverse, cur[...])


def local_call(kernel, out_shapes, name, *args):
    return pl.pallas_call(
        kernel,
        out_shape=out_shapes,
        compiler_params=pltpu.CompilerParams(vmem_limit_bytes=VMEM_LIMIT),
        name=name,
    )(*args)


def per_device(n, right_sides, diag_shift, near_block, cluster_basis, couplings, partner, owned_count):
    cols = right_sides.shape[1]
    square = jax.ShapeDtypeStruct((cols, cols), jnp.float32)
    slots = partner.shape[1]
    live = jnp.arange(slots) < owned_count[0]
    where_to = partner[0] % GROUP
    match = jnp.logical_and(live[None, :], where_to[None, :] == jnp.arange(GROUP)[:, None])
    pad = [(0, GROUP - slots)]
    meta = jnp.stack([
        jnp.argmax(match, axis=1).astype(jnp.int32),
        jnp.any(match, axis=1).astype(jnp.int32),
        jnp.pad(where_to.astype(jnp.int32), pad),
        jnp.pad(live.astype(jnp.int32), pad),
    ])

    def coefficients(vectors):
        return lax.dot_general(vectors, cluster_basis, contract_first, precision=high)

    def image_of(vectors, far_t):
        near = jnp.dot(near_block, vectors, precision=high)
        far = lax.dot_general(cluster_basis, far_t, contract_last, precision=high)
        return diag_shift[:, None] * vectors + (near + far)

    def gram(x, y):
        return lax.dot_general(x, y, contract_first, precision=highest)

    far_b = far_exchange(n, meta, coefficients(right_sides), couplings)
    image = image_of(right_sides, far_b)
    local = jnp.concatenate([
        gram(right_sides, right_sides), gram(right_sides, image), gram(image, image)])
    far_w, alpha, beta, updated = far_exchange(n, meta, coefficients(image), couplings, local)
    residual = right_sides - jnp.dot(image, alpha, precision=highest)
    direction = residual + jnp.dot(right_sides, beta, precision=highest)
    far_d = far_b + (gram(beta, far_b) - gram(alpha, far_w))
    image2 = image_of(direction, far_d)
    curvature = sum_all(n, gram(direction, image2), 2)
    alpha2 = local_call(second_kernel, square, "second_step", curvature, updated)
    answer = jnp.dot(right_sides, alpha, precision=highest) + jnp.dot(direction, alpha2, precision=highest)
    residual = residual - jnp.dot(image2, alpha2, precision=highest)
    return answer, residual


def solution(mesh):
    n = mesh.shape["clu"]
    in_specs = (
        P("clu", None),
        P("clu"),
        P("clu", None),
        P("clu", None),
        P("clu", None, None),
        P("clu", None),
        P("clu"),
    )
    out_specs = (P("clu", None), P("clu", None))
    return jax.shard_map(
        functools.partial(per_device, n), mesh=mesh, in_specs=in_specs,
        out_specs=out_specs, check_vma=False)
```

```python
import functools

import jax
import jax.numpy as jnp
from jax import lax
from jax.experimental import pallas as pl
from jax.experimental.pallas import tpu as pltpu
from jax.sharding import PartitionSpec as P

GROUP = 8
MESH = pl.DeviceIdType.MESH
VMEM_LIMIT = 56 * 1024 * 1024

highest = lax.Precision.HIGHEST
high = lax.Precision.HIGH
contract_first = (((0,), (0,)), ((), ()))
contract_last = (((1,), (1,)), ((), ()))
plain = (((1,), (0,)), ((), ()))


def split(x):
    hi = x.astype(jnp.bfloat16)
    return hi, (x - hi.astype(jnp.float32)).astype(jnp.bfloat16)


def dot3(a, b, dims):
    a_hi, a_lo = a
    b_hi, b_lo = b
    d = functools.partial(
        lax.dot_general, dimension_numbers=dims, preferred_element_type=jnp.float32
    )
    return d(a_hi, b_hi) + (d(a_hi, b_lo) + d(a_lo, b_hi))


def far_kernel(n, solve, *refs):
    if solve:
        meta, coef, c_hbm, grams, gram0, inverse0, out, alpha, beta, updated = refs[:10]
        refs = refs[10:]
    else:
        meta, coef, c_hbm, grams, out, gram0, inverse0 = refs[:7]
        refs = refs[7:]
    cv, ahead, ret, rs, ri, up, rz, c_sem, fs, fr, ss, sr, xs, xr, zs, zr = refs[:16]
    me = lax.axis_index("clu")
    z = me // GROUP
    p = me % GROUP
    a = p // 2
    k = p % 2
    base = z * GROUP
    has_up = z < n // GROUP - 1
    has_down = z > 0
    sib = base + (p + 1 - 2 * k)
    psib = p + 1 - 2 * k
    slots = cv.shape[0]

    def chip(i):
        x, y = a % 2, a // 2
        nx = 1 - x if i & 1 else x
        ny = 1 - y if i & 2 else y
        return ny * 2 + nx

    chips = {i: chip(i) for i in (1, 2, 3)}

    def rc(src, dst, ssem, rsem, dev):
        return pltpu.make_async_remote_copy(
            src_ref=src, dst_ref=dst, send_sem=ssem, recv_sem=rsem,
            device_id=(dev,), device_id_type=MESH)

    c_copy = pltpu.make_async_copy(c_hbm, cv, c_sem)
    c_copy.start()

    @pl.when(jnp.logical_not(has_up))
    def _():
        def zero(j, c):
            ahead[j] = jnp.zeros(ahead.shape[1:], jnp.float32)
            return c
        lax.fori_loop(0, GROUP, zero, 0)

    greet_all(n, me)

    f_z = rc(coef, ahead.at[p], fs.at[0], fr.at[0], me - GROUP)

    def f_own(i):
        return rc(coef, ahead.at[p], fs.at[i], fr.at[i], base + chips[i] * 2 + k)

    def f_upper(i):
        return rc(ahead.at[p], ahead.at[p], fs.at[i], fr.at[i], base + chips[i] * 2 + k)

    def f_in(i):
        t = chips[i] * 2 + k
        return rc(ahead.at[t], ahead.at[t], fs.at[3 + i], fr.at[i], sib)

    def f_sib(i):
        t = chips[i] * 2 + k
        return rc(ahead.at[t], ahead.at[t], fs.at[3 + i], fr.at[3 + i], sib)

    def f_sib_in(i):
        t = chips[i] * 2 + 1 - k
        return rc(ahead.at[t], ahead.at[t], fs.at[3 + i], fr.at[3 + i], sib)

    f_s_own = rc(coef, ahead.at[p], fs.at[7], fr.at[7], sib)
    f_s_upper = rc(ahead.at[p], ahead.at[p], fs.at[7], fr.at[7], sib)
    f_s_in = rc(ahead.at[psib], ahead.at[psib], fs.at[7], fr.at[7], sib)

    @pl.when(has_down)
    def _():
        f_z.start()

    for i in (3, 1, 2):
        @pl.when(chips[i] < a)
        def _(i=i):
            f_own(i).start()

    @pl.when(k == 1)
    def _():
        f_s_own.start()

    total = refs[16]
    finish_sum, drain_sum = start_sum(n, me, grams, total, *refs[17:])

    c_copy.wait()

    def back(t, carry):
        s = meta[0, t]
        term = dot3(split(coef[...]), split(cv[s]), plain)
        ret[t] = jnp.where(meta[1, t] > 0, term, 0.0)
        return carry

    lax.fori_loop(0, GROUP, back, 0)

    r_s = [rc(ret.at[psib], rs.at[0], ss.at[0], sr.at[0], sib)]
    for i in (1, 2, 3):
        r_s.append(rc(ret.at[chips[i] * 2 + 1 - k], rs.at[i], ss.at[i], sr.at[i], sib))
    for i in (3, 1, 2, 0):
        r_s[i].start()

    @pl.when(has_up)
    def _():
        f_z.wait_recv()
        for i in (3, 1, 2):
            @pl.when(chips[i] > a)
            def _(i=i):
                f_upper(i).start()

        @pl.when(k == 0)
        def _():
            f_s_upper.start()

    r_x = [None]
    for i in (1, 2, 3):
        r_x.append(rc(ret.at[chips[i] * 2 + k], ri.at[i - 1], xs.at[i - 1], xr.at[i - 1],
                      base + chips[i] * 2 + k))
    for i in (3, 1, 2):
        r_s[i].wait_recv()
        t = chips[i] * 2 + k
        ret[t] = ret[t] + rs[i]
        r_x[i].start()

    finish_sum()
    if solve:
        first_steps(total, gram0, inverse0, alpha, beta, updated)
    else:
        g0 = symmetric(total[...])
        gram0[...] = g0
        inverse0[...] = invert([g0])[0]

    for i in (1, 2, 3):
        @pl.when(jnp.logical_or(chips[i] > a, has_up))
        def _(i=i):
            f_in(i).wait_recv()
            f_sib(i).start()

    r_s[0].wait_recv()
    up[...] = ret[p] + jnp.where(k == 0, rs[0], 0.0)
    out[...] = jnp.where(k == 0, 0.0, rs[0])
    for i in (1, 2, 3):
        r_x[i].wait_recv()
        mine = chips[i] < a
        got = ri[i - 1]
        up[...] += jnp.where(mine, 0.0, got)
        out[...] += jnp.where(mine, got, 0.0)
    r_z = rc(up, rz, zs, zr, me + GROUP)

    @pl.when(has_up)
    def _():
        r_z.start()

    for i in (1, 2, 3):
        @pl.when(jnp.logical_or(chips[i] > a, has_up))
        def _(i=i):
            f_sib_in(i).wait_recv()

    @pl.when(jnp.logical_or(k == 0, has_up))
    def _():
        f_s_in.wait_recv()

    def forth(s, carry):
        block = ahead[meta[2, s]]
        term = dot3(split(block), split(cv[s]), contract_last)
        out[...] += jnp.where(meta[3, s] > 0, term, 0.0)
        return carry

    lax.fori_loop(0, slots, forth, 0)

    @pl.when(has_down)
    def _():
        r_z.wait_recv()
        out[...] += rz[...]
        f_z.wait_send()

    for i in (1, 2, 3):
        @pl.when(jnp.logical_or(chips[i] < a, has_up))
        def _(i=i):
            f_own(i).wait_send()

        @pl.when(jnp.logical_or(chips[i] > a, has_up))
        def _(i=i):
            f_sib(i).wait_send()

        r_x[i].wait_send()
    for i in range(4):
        r_s[i].wait_send()

    @pl.when(jnp.logical_or(k == 1, has_up))
    def _():
        f_s_own.wait_send()

    @pl.when(has_up)
    def _():
        r_z.wait_send()

    drain_sum()


def far_exchange(n, meta, coef_t, couplings, grams, *first):
    blk = coef_t.shape
    f32 = jnp.float32
    solve = len(first) > 0
    vmem = pl.BlockSpec(memory_space=pltpu.VMEM)
    one = jax.ShapeDtypeStruct(blk, f32)
    square = jax.ShapeDtypeStruct((grams.shape[1],) * 2, f32)
    outs = (one,) + (square,) * (3 if solve else 2)
    extra = [pltpu.VMEM(grams.shape, f32)] + sum_scratch(n, grams)
    return pl.pallas_call(
        functools.partial(far_kernel, n, solve),
        out_shape=outs,
        in_specs=[
            pl.BlockSpec(memory_space=pltpu.SMEM),
            pl.BlockSpec(memory_space=pltpu.VMEM),
            pl.BlockSpec(memory_space=pl.ANY),
        ] + [vmem] * (1 + len(first)),
        out_specs=(vmem,) * len(outs),
        scratch_shapes=[
            pltpu.VMEM(couplings.shape, f32),
            pltpu.VMEM((GROUP,) + blk, f32),
            pltpu.VMEM((GROUP,) + blk, f32),
            pltpu.VMEM((4,) + blk, f32),
            pltpu.VMEM((3,) + blk, f32),
            pltpu.VMEM(blk, f32),
            pltpu.VMEM(blk, f32),
            pltpu.SemaphoreType.DMA,
            pltpu.SemaphoreType.DMA((8,)),
            pltpu.SemaphoreType.DMA((8,)),
            pltpu.SemaphoreType.DMA((4,)),
            pltpu.SemaphoreType.DMA((4,)),
            pltpu.SemaphoreType.DMA((3,)),
            pltpu.SemaphoreType.DMA((3,)),
            pltpu.SemaphoreType.DMA,
            pltpu.SemaphoreType.DMA,
        ] + extra,
        compiler_params=pltpu.CompilerParams(
            collective_id=int(solve), has_side_effects=True, vmem_limit_bytes=VMEM_LIMIT),
        name="far_exchange_solve" if solve else "far_exchange",
    )(meta, coef_t, couplings, grams, *first)


def greet_all(n, me):
    base, p, groups = me // GROUP * GROUP, me % GROUP, n // GROUP
    barrier = pltpu.get_barrier_semaphore()
    for j in range(1, GROUP):
        pl.semaphore_signal(barrier, inc=1, device_id=(base + (p + j) % GROUP,), device_id_type=MESH)
    for j in range(1, groups):
        pl.semaphore_signal(barrier, inc=1, device_id=((me + j * GROUP) % n,), device_id_type=MESH)
    pl.semaphore_wait(barrier, GROUP - 1 + groups - 1)


def start_sum(n, me, g, out, inbox, planes, s1, r1, s2, r2, s3, r3):
    z = me // GROUP
    p = me % GROUP
    base = z * GROUP
    groups = n // GROUP
    rows = g.shape[0] // GROUP
    pending = []

    def rc(src, dst, ssem, rsem, dev):
        return pltpu.make_async_remote_copy(
            src_ref=src, dst_ref=dst, send_sem=ssem, recv_sem=rsem,
            device_id=(dev,), device_id_type=MESH)

    def part(t):
        return pl.ds(pl.multiple_of(t * rows, 8), rows)

    for j in range(1, GROUP):
        t = (p + j) % GROUP
        pending.append(rc(g.at[part(t)], inbox.at[j - 1], s1.at[j - 1], r1.at[j - 1], base + t))
        pending[-1].start()
    scatter = list(pending)

    def finish():
        total = g[part(p), :]
        for j in range(1, GROUP):
            scatter[j - 1].wait_recv()
            total = total + inbox[j - 1]
        planes[z] = total
        for j in range(1, groups):
            pending.append(rc(planes.at[z], planes.at[z], s2.at[j - 1], r2.at[j - 1], (me + j * GROUP) % n))
            pending[-1].start()
        for j in range(1, groups):
            src = (z + groups - j) % groups
            rc(planes.at[src], planes.at[src], s2.at[j - 1], r2.at[j - 1], (me + j * GROUP) % n).wait_recv()
        total = planes[0]
        for j in range(1, groups):
            total = total + planes[j]
        out[part(p), :] = total
        for j in range(1, GROUP):
            t = (p + j) % GROUP
            pending.append(rc(out.at[part(p)], out.at[part(p)], s3.at[j - 1], r3.at[j - 1], base + t))
            pending[-1].start()
        for j in range(1, GROUP):
            t = (p + GROUP - j) % GROUP
            rc(out.at[part(t)], out.at[part(t)], s3.at[j - 1], r3.at[j - 1], base + t).wait_recv()

    def drain():
        for copy in pending:
            copy.wait_send()

    return finish, drain


def sum_kernel(n, g, out, *refs):
    me = lax.axis_index("clu")
    greet_all(n, me)
    finish, drain = start_sum(n, me, g, out, *refs)
    finish()
    drain()


def sum_scratch(n, g):
    rows, groups = g.shape[0] // GROUP, n // GROUP
    counts = (GROUP - 1, GROUP - 1, groups - 1, groups - 1, GROUP - 1, GROUP - 1)
    return [
        pltpu.VMEM((GROUP - 1, rows, g.shape[1]), jnp.float32),
        pltpu.VMEM((groups, rows, g.shape[1]), jnp.float32),
    ] + [pltpu.SemaphoreType.DMA((c,)) for c in counts]


def sum_all(n, g, collective_id):
    f32 = jnp.float32
    return pl.pallas_call(
        functools.partial(sum_kernel, n),
        out_shape=jax.ShapeDtypeStruct(g.shape, f32),
        in_specs=[pl.BlockSpec(memory_space=pltpu.VMEM)],
        out_specs=pl.BlockSpec(memory_space=pltpu.VMEM),
        scratch_shapes=sum_scratch(n, g),
        compiler_params=pltpu.CompilerParams(
            collective_id=collective_id, has_side_effects=True, vmem_limit_bytes=VMEM_LIMIT),
        name="sum_all_%d" % g.shape[0],
    )(g)


def mm(x, y, dims=plain):
    return lax.dot_general(x, y, dims, precision=highest, preferred_element_type=jnp.float32)


def invert_blocks(mats):
    size = mats[0].shape[0]
    lane = lax.broadcasted_iota(jnp.int32, (1, size), 1)
    sub = lax.broadcasted_iota(jnp.int32, (size, 1), 0)
    unroll = 8

    def body(_, state):
        state = list(state)
        for step in range(unroll):
            for m, mat in enumerate(state):
                row = mat[step:step + 1, :]
                col = mat[:, step:step + 1]
                inv = 1.0 / mat[step:step + 1, step:step + 1]
                scaled = jnp.where(lane == step, inv, row * inv)
                factor = jnp.where(sub == step, -1.0, col)
                kept = jnp.where(jnp.logical_or(lane == step, sub == step), 0.0, mat)
                state[m] = kept - factor * scaled
        state = [jnp.concatenate([x[unroll:], x[:unroll]], axis=0) for x in state]
        return tuple(pltpu.roll(x, size - unroll, 1) for x in state)

    return list(lax.fori_loop(0, size // unroll, body, tuple(mats)))


def invert(mats):
    half = mats[0].shape[0] // 2
    a = [m[:half, :half] for m in mats]
    b = [m[:half, half:] for m in mats]
    d = [m[half:, half:] for m in mats]
    ai = invert_blocks(a)
    ab = [mm(x, y) for x, y in zip(ai, b)]
    si = invert_blocks([x - mm(y, w, contract_first) for x, y, w in zip(d, b, ab)])
    result = []
    for x, y, w in zip(ai, ab, si):
        yw = mm(y, w)
        top = jnp.concatenate([x + mm(yw, y, contract_last), -yw], axis=1)
        low = jnp.concatenate([-jnp.transpose(yw), w], axis=1)
        result.append(jnp.concatenate([top, low], axis=0))
    return result


def symmetric(matrix):
    return 0.5 * (matrix + jnp.transpose(matrix))


def first_steps(grams, gram0, inverse0, alpha_ref, beta_ref, updated_ref):
    size = grams.shape[1]
    g0 = gram0[...]
    g1 = symmetric(grams[:size, :])
    g2 = symmetric(grams[size:, :])
    (i1,) = invert([g1])
    alpha = mm(i1, g0)
    alpha_ref[...] = alpha
    inner = mm(g2, alpha) - g1
    cross = mm(g1, alpha)
    updated = symmetric((g0 - cross) + mm(alpha, inner, contract_first))
    updated_ref[...] = updated
    beta_ref[...] = mm(inverse0[...], updated)


def second_kernel(curv, cur, alpha_ref):
    (inverse,) = invert([symmetric(curv[...])])
    alpha_ref[...] = mm(inverse, cur[...])


def local_call(kernel, out_shapes, name, *args):
    return pl.pallas_call(
        kernel,
        out_shape=out_shapes,
        compiler_params=pltpu.CompilerParams(vmem_limit_bytes=VMEM_LIMIT),
        name=name,
    )(*args)


def per_device(n, right_sides, diag_shift, near_block, cluster_basis, couplings, partner, owned_count):
    cols = right_sides.shape[1]
    square = jax.ShapeDtypeStruct((cols, cols), jnp.float32)
    slots = partner.shape[1]
    live = jnp.arange(slots) < owned_count[0]
    where_to = partner[0] % GROUP
    match = jnp.logical_and(live[None, :], where_to[None, :] == jnp.arange(GROUP)[:, None])
    pad = [(0, GROUP - slots)]
    meta = jnp.stack([
        jnp.argmax(match, axis=1).astype(jnp.int32),
        jnp.any(match, axis=1).astype(jnp.int32),
        jnp.pad(where_to.astype(jnp.int32), pad),
        jnp.pad(live.astype(jnp.int32), pad),
    ])

    def coefficients(vectors):
        return lax.dot_general(vectors, cluster_basis, contract_first, precision=high)

    def image_of(vectors, far_t):
        near = jnp.dot(near_block, vectors, precision=high)
        far = lax.dot_general(cluster_basis, far_t, contract_last, precision=high)
        return diag_shift[:, None] * vectors + (near + far)

    def gram(x, y):
        return lax.dot_general(x, y, contract_first, precision=highest)

    far_b, gram0, inverse0 = far_exchange(
        n, meta, coefficients(right_sides), couplings, gram(right_sides, right_sides))
    image = image_of(right_sides, far_b)
    local = jnp.concatenate([gram(right_sides, image), gram(image, image)])
    far_w, alpha, beta, updated = far_exchange(
        n, meta, coefficients(image), couplings, local, gram0, inverse0)
    residual = right_sides - jnp.dot(image, alpha, precision=highest)
    direction = residual + jnp.dot(right_sides, beta, precision=highest)
    far_d = far_b + (gram(beta, far_b) - gram(alpha, far_w))
    image2 = image_of(direction, far_d)
    curvature = sum_all(n, gram(direction, image2), 2)
    alpha2 = local_call(second_kernel, square, "second_step", curvature, updated)
    answer = jnp.dot(right_sides, alpha, precision=highest) + jnp.dot(direction, alpha2, precision=highest)
    residual = residual - jnp.dot(image2, alpha2, precision=highest)
    return answer, residual


def solution(mesh):
    n = mesh.shape["clu"]
    in_specs = (
        P("clu", None),
        P("clu"),
        P("clu", None),
        P("clu", None),
        P("clu", None, None),
        P("clu", None),
        P("clu"),
    )
    out_specs = (P("clu", None), P("clu", None))
    return jax.shard_map(
        functools.partial(per_device, n), mesh=mesh, in_specs=in_specs,
        out_specs=out_specs, check_vma=False)
```

```python
import functools

import jax
import jax.numpy as jnp
from jax import lax
from jax.experimental import pallas as pl
from jax.experimental.pallas import tpu as pltpu
from jax.sharding import PartitionSpec as P

GROUP = 8
MESH = pl.DeviceIdType.MESH
VMEM_LIMIT = 56 * 1024 * 1024

highest = lax.Precision.HIGHEST
high = lax.Precision.HIGH
contract_first = (((0,), (0,)), ((), ()))
contract_last = (((1,), (1,)), ((), ()))
plain = (((1,), (0,)), ((), ()))


def split(x):
    hi = x.astype(jnp.bfloat16)
    return hi, (x - hi.astype(jnp.float32)).astype(jnp.bfloat16)


def dot3(a, b, dims):
    a_hi, a_lo = a
    b_hi, b_lo = b
    d = functools.partial(
        lax.dot_general, dimension_numbers=dims, preferred_element_type=jnp.float32
    )
    return d(a_hi, b_hi) + (d(a_hi, b_lo) + d(a_lo, b_hi))


def far_kernel(n, solve, *refs):
    if solve:
        meta, coef, c_hbm, grams, out, alpha, beta, updated = refs[:8]
        refs = refs[8:]
    else:
        meta, coef, c_hbm, out = refs[:4]
        refs = refs[4:]
    cv, ahead, ret, rs, ri, up, rz, c_sem, fs, fr, ss, sr, xs, xr, zs, zr = refs[:16]
    me = lax.axis_index("clu")
    z = me // GROUP
    p = me % GROUP
    a = p // 2
    k = p % 2
    base = z * GROUP
    has_up = z < n // GROUP - 1
    has_down = z > 0
    sib = base + (p + 1 - 2 * k)
    psib = p + 1 - 2 * k
    slots = cv.shape[0]

    def chip(i):
        x, y = a % 2, a // 2
        nx = 1 - x if i & 1 else x
        ny = 1 - y if i & 2 else y
        return ny * 2 + nx

    chips = {i: chip(i) for i in (1, 2, 3)}

    def rc(src, dst, ssem, rsem, dev):
        return pltpu.make_async_remote_copy(
            src_ref=src, dst_ref=dst, send_sem=ssem, recv_sem=rsem,
            device_id=(dev,), device_id_type=MESH)

    c_copy = pltpu.make_async_copy(c_hbm, cv, c_sem)
    c_copy.start()

    @pl.when(jnp.logical_not(has_up))
    def _():
        def zero(j, c):
            ahead[j] = jnp.zeros(ahead.shape[1:], jnp.float32)
            return c
        lax.fori_loop(0, GROUP, zero, 0)

    if solve:
        greet_all(n, me)
    else:
        barrier = pltpu.get_barrier_semaphore()
        pl.semaphore_signal(barrier, inc=1, device_id=(sib,), device_id_type=MESH)
        for i in (1, 2, 3):
            pl.semaphore_signal(barrier, inc=1, device_id=(base + chips[i] * 2 + k,), device_id_type=MESH)

        @pl.when(has_up)
        def _():
            pl.semaphore_signal(barrier, inc=1, device_id=(me + GROUP,), device_id_type=MESH)

        @pl.when(has_down)
        def _():
            pl.semaphore_signal(barrier, inc=1, device_id=(me - GROUP,), device_id_type=MESH)

        pl.semaphore_wait(barrier, 4 + jnp.where(has_up, 1, 0) + jnp.where(has_down, 1, 0))

    f_z = rc(coef, ahead.at[p], fs.at[0], fr.at[0], me - GROUP)

    def f_own(i):
        return rc(coef, ahead.at[p], fs.at[i], fr.at[i], base + chips[i] * 2 + k)

    def f_upper(i):
        return rc(ahead.at[p], ahead.at[p], fs.at[i], fr.at[i], base + chips[i] * 2 + k)

    def f_in(i):
        t = chips[i] * 2 + k
        return rc(ahead.at[t], ahead.at[t], fs.at[3 + i], fr.at[i], sib)

    def f_sib(i):
        t = chips[i] * 2 + k
        return rc(ahead.at[t], ahead.at[t], fs.at[3 + i], fr.at[3 + i], sib)

    def f_sib_in(i):
        t = chips[i] * 2 + 1 - k
        return rc(ahead.at[t], ahead.at[t], fs.at[3 + i], fr.at[3 + i], sib)

    f_s_own = rc(coef, ahead.at[p], fs.at[7], fr.at[7], sib)
    f_s_upper = rc(ahead.at[p], ahead.at[p], fs.at[7], fr.at[7], sib)
    f_s_in = rc(ahead.at[psib], ahead.at[psib], fs.at[7], fr.at[7], sib)

    @pl.when(has_down)
    def _():
        f_z.start()

    for i in (3, 1, 2):
        @pl.when(chips[i] < a)
        def _(i=i):
            f_own(i).start()

    @pl.when(k == 1)
    def _():
        f_s_own.start()

    if solve:
        total = refs[16]
        finish_sum, drain_sum = start_sum(n, me, grams, total, *refs[17:])

    c_copy.wait()

    def back(t, carry):
        s = meta[0, t]
        term = dot3(split(coef[...]), split(cv[s]), plain)
        ret[t] = jnp.where(meta[1, t] > 0, term, 0.0)
        return carry

    lax.fori_loop(0, GROUP, back, 0)

    r_s = [rc(ret.at[psib], rs.at[0], ss.at[0], sr.at[0], sib)]
    for i in (1, 2, 3):
        r_s.append(rc(ret.at[chips[i] * 2 + 1 - k], rs.at[i], ss.at[i], sr.at[i], sib))
    for i in (3, 1, 2, 0):
        r_s[i].start()

    @pl.when(has_up)
    def _():
        f_z.wait_recv()
        for i in (3, 1, 2):
            @pl.when(chips[i] > a)
            def _(i=i):
                f_upper(i).start()

        @pl.when(k == 0)
        def _():
            f_s_upper.start()

    r_x = [None]
    for i in (1, 2, 3):
        r_x.append(rc(ret.at[chips[i] * 2 + k], ri.at[i - 1], xs.at[i - 1], xr.at[i - 1],
                      base + chips[i] * 2 + k))
    for i in (3, 1, 2):
        r_s[i].wait_recv()
        t = chips[i] * 2 + k
        ret[t] = ret[t] + rs[i]
        r_x[i].start()

    if solve:
        finish_sum()

    for i in (1, 2, 3):
        @pl.when(jnp.logical_or(chips[i] > a, has_up))
        def _(i=i):
            f_in(i).wait_recv()
            f_sib(i).start()

    r_s[0].wait_recv()
    up[...] = ret[p] + jnp.where(k == 0, rs[0], 0.0)
    out[...] = jnp.where(k == 0, 0.0, rs[0])
    for i in (1, 2, 3):
        r_x[i].wait_recv()
        mine = chips[i] < a
        got = ri[i - 1]
        up[...] += jnp.where(mine, 0.0, got)
        out[...] += jnp.where(mine, got, 0.0)
    r_z = rc(up, rz, zs, zr, me + GROUP)

    @pl.when(has_up)
    def _():
        r_z.start()

    if solve:
        first_kernel(total, alpha, beta, updated)

    for i in (1, 2, 3):
        @pl.when(jnp.logical_or(chips[i] > a, has_up))
        def _(i=i):
            f_sib_in(i).wait_recv()

    @pl.when(jnp.logical_or(k == 0, has_up))
    def _():
        f_s_in.wait_recv()

    def forth(s, carry):
        block = ahead[meta[2, s]]
        term = dot3(split(block), split(cv[s]), contract_last)
        out[...] += jnp.where(meta[3, s] > 0, term, 0.0)
        return carry

    lax.fori_loop(0, slots, forth, 0)

    @pl.when(has_down)
    def _():
        r_z.wait_recv()
        out[...] += rz[...]
        f_z.wait_send()

    for i in (1, 2, 3):
        @pl.when(jnp.logical_or(chips[i] < a, has_up))
        def _(i=i):
            f_own(i).wait_send()

        @pl.when(jnp.logical_or(chips[i] > a, has_up))
        def _(i=i):
            f_sib(i).wait_send()

        r_x[i].wait_send()
    for i in range(4):
        r_s[i].wait_send()

    @pl.when(jnp.logical_or(k == 1, has_up))
    def _():
        f_s_own.wait_send()

    @pl.when(has_up)
    def _():
        r_z.wait_send()

    if solve:
        drain_sum()


def far_exchange(n, meta, coef_t, couplings, grams=None):
    blk = coef_t.shape
    f32 = jnp.float32
    solve = grams is not None
    vmem = pl.BlockSpec(memory_space=pltpu.VMEM)
    one = jax.ShapeDtypeStruct(blk, f32)
    extra = []
    if solve:
        square = jax.ShapeDtypeStruct((grams.shape[1],) * 2, f32)
        extra = [pltpu.VMEM(grams.shape, f32)] + sum_scratch(n, grams)
    return pl.pallas_call(
        functools.partial(far_kernel, n, solve),
        out_shape=(one, square, square, square) if solve else one,
        in_specs=[
            pl.BlockSpec(memory_space=pltpu.SMEM),
            pl.BlockSpec(memory_space=pltpu.VMEM),
            pl.BlockSpec(memory_space=pl.ANY),
        ] + [vmem] * solve,
        out_specs=(vmem,) * 4 if solve else vmem,
        scratch_shapes=[
            pltpu.VMEM(couplings.shape, f32),
            pltpu.VMEM((GROUP,) + blk, f32),
            pltpu.VMEM((GROUP,) + blk, f32),
            pltpu.VMEM((4,) + blk, f32),
            pltpu.VMEM((3,) + blk, f32),
            pltpu.VMEM(blk, f32),
            pltpu.VMEM(blk, f32),
            pltpu.SemaphoreType.DMA,
            pltpu.SemaphoreType.DMA((8,)),
            pltpu.SemaphoreType.DMA((8,)),
            pltpu.SemaphoreType.DMA((4,)),
            pltpu.SemaphoreType.DMA((4,)),
            pltpu.SemaphoreType.DMA((3,)),
            pltpu.SemaphoreType.DMA((3,)),
            pltpu.SemaphoreType.DMA,
            pltpu.SemaphoreType.DMA,
        ] + extra,
        compiler_params=pltpu.CompilerParams(
            collective_id=int(solve), has_side_effects=True, vmem_limit_bytes=VMEM_LIMIT),
        name="far_exchange_solve" if solve else "far_exchange",
    )(meta, coef_t, couplings, *([grams] if solve else []))


def greet_all(n, me):
    base, p, groups = me // GROUP * GROUP, me % GROUP, n // GROUP
    barrier = pltpu.get_barrier_semaphore()
    for j in range(1, GROUP):
        pl.semaphore_signal(barrier, inc=1, device_id=(base + (p + j) % GROUP,), device_id_type=MESH)
    for j in range(1, groups):
        pl.semaphore_signal(barrier, inc=1, device_id=((me + j * GROUP) % n,), device_id_type=MESH)
    pl.semaphore_wait(barrier, GROUP - 1 + groups - 1)


def start_sum(n, me, g, out, inbox, planes, s1, r1, s2, r2, s3, r3):
    z = me // GROUP
    p = me % GROUP
    base = z * GROUP
    groups = n // GROUP
    rows = g.shape[0] // GROUP
    pending = []

    def rc(src, dst, ssem, rsem, dev):
        return pltpu.make_async_remote_copy(
            src_ref=src, dst_ref=dst, send_sem=ssem, recv_sem=rsem,
            device_id=(dev,), device_id_type=MESH)

    def part(t):
        return pl.ds(pl.multiple_of(t * rows, 8), rows)

    for j in range(1, GROUP):
        t = (p + j) % GROUP
        pending.append(rc(g.at[part(t)], inbox.at[j - 1], s1.at[j - 1], r1.at[j - 1], base + t))
        pending[-1].start()
    scatter = list(pending)

    def finish():
        total = g[part(p), :]
        for j in range(1, GROUP):
            scatter[j - 1].wait_recv()
            total = total + inbox[j - 1]
        planes[z] = total
        for j in range(1, groups):
            pending.append(rc(planes.at[z], planes.at[z], s2.at[j - 1], r2.at[j - 1], (me + j * GROUP) % n))
            pending[-1].start()
        for j in range(1, groups):
            src = (z + groups - j) % groups
            rc(planes.at[src], planes.at[src], s2.at[j - 1], r2.at[j - 1], (me + j * GROUP) % n).wait_recv()
        total = planes[0]
        for j in range(1, groups):
            total = total + planes[j]
        out[part(p), :] = total
        for j in range(1, GROUP):
            t = (p + j) % GROUP
            pending.append(rc(out.at[part(p)], out.at[part(p)], s3.at[j - 1], r3.at[j - 1], base + t))
            pending[-1].start()
        for j in range(1, GROUP):
            t = (p + GROUP - j) % GROUP
            rc(out.at[part(t)], out.at[part(t)], s3.at[j - 1], r3.at[j - 1], base + t).wait_recv()

    def drain():
        for copy in pending:
            copy.wait_send()

    return finish, drain


def sum_kernel(n, g, out, *refs):
    me = lax.axis_index("clu")
    greet_all(n, me)
    finish, drain = start_sum(n, me, g, out, *refs)
    finish()
    drain()


def sum_scratch(n, g):
    rows, groups = g.shape[0] // GROUP, n // GROUP
    counts = (GROUP - 1, GROUP - 1, groups - 1, groups - 1, GROUP - 1, GROUP - 1)
    return [
        pltpu.VMEM((GROUP - 1, rows, g.shape[1]), jnp.float32),
        pltpu.VMEM((groups, rows, g.shape[1]), jnp.float32),
    ] + [pltpu.SemaphoreType.DMA((c,)) for c in counts]


def sum_all(n, g, collective_id):
    f32 = jnp.float32
    return pl.pallas_call(
        functools.partial(sum_kernel, n),
        out_shape=jax.ShapeDtypeStruct(g.shape, f32),
        in_specs=[pl.BlockSpec(memory_space=pltpu.VMEM)],
        out_specs=pl.BlockSpec(memory_space=pltpu.VMEM),
        scratch_shapes=sum_scratch(n, g),
        compiler_params=pltpu.CompilerParams(
            collective_id=collective_id, has_side_effects=True, vmem_limit_bytes=VMEM_LIMIT),
        name="sum_all_%d" % g.shape[0],
    )(g)


def mm(x, y, dims=plain):
    return lax.dot_general(x, y, dims, precision=highest, preferred_element_type=jnp.float32)


def invert_blocks(mats):
    size = mats[0].shape[0]
    lane = lax.broadcasted_iota(jnp.int32, (1, size), 1)
    sub = lax.broadcasted_iota(jnp.int32, (size, 1), 0)
    unroll = 8

    def body(_, state):
        state = list(state)
        for step in range(unroll):
            for m, mat in enumerate(state):
                row = mat[step:step + 1, :]
                col = mat[:, step:step + 1]
                inv = 1.0 / mat[step:step + 1, step:step + 1]
                scaled = jnp.where(lane == step, inv, row * inv)
                factor = jnp.where(sub == step, -1.0, col)
                kept = jnp.where(jnp.logical_or(lane == step, sub == step), 0.0, mat)
                state[m] = kept - factor * scaled
        state = [jnp.concatenate([x[unroll:], x[:unroll]], axis=0) for x in state]
        return tuple(pltpu.roll(x, size - unroll, 1) for x in state)

    return list(lax.fori_loop(0, size // unroll, body, tuple(mats)))


def invert(mats):
    half = mats[0].shape[0] // 2
    a = [m[:half, :half] for m in mats]
    b = [m[:half, half:] for m in mats]
    d = [m[half:, half:] for m in mats]
    ai = invert_blocks(a)
    ab = [mm(x, y) for x, y in zip(ai, b)]
    si = invert_blocks([x - mm(y, w, contract_first) for x, y, w in zip(d, b, ab)])
    result = []
    for x, y, w in zip(ai, ab, si):
        yw = mm(y, w)
        top = jnp.concatenate([x + mm(yw, y, contract_last), -yw], axis=1)
        low = jnp.concatenate([-jnp.transpose(yw), w], axis=1)
        result.append(jnp.concatenate([top, low], axis=0))
    return result


def symmetric(matrix):
    return 0.5 * (matrix + jnp.transpose(matrix))


def first_kernel(grams, alpha_ref, beta_ref, updated_ref):
    size = grams.shape[1]
    g0 = symmetric(grams[:size, :])
    g1 = symmetric(grams[size:2 * size, :])
    g2 = symmetric(grams[2 * size:, :])
    i0, i1 = invert([g0, g1])
    alpha = mm(i1, g0)
    alpha_ref[...] = alpha
    inner = mm(g2, alpha) - g1
    cross = mm(g1, alpha)
    updated = symmetric((g0 - cross) + mm(alpha, inner, contract_first))
    updated_ref[...] = updated
    beta_ref[...] = mm(i0, updated)


def second_kernel(curv, cur, alpha_ref):
    (inverse,) = invert([symmetric(curv[...])])
    alpha_ref[...] = mm(inverse, cur[...])


def local_call(kernel, out_shapes, name, *args):
    return pl.pallas_call(
        kernel,
        out_shape=out_shapes,
        compiler_params=pltpu.CompilerParams(vmem_limit_bytes=VMEM_LIMIT),
        name=name,
    )(*args)


def per_device(n, right_sides, diag_shift, near_block, cluster_basis, couplings, partner, owned_count):
    cols = right_sides.shape[1]
    square = jax.ShapeDtypeStruct((cols, cols), jnp.float32)
    slots = partner.shape[1]
    live = jnp.arange(slots) < owned_count[0]
    where_to = partner[0] % GROUP
    match = jnp.logical_and(live[None, :], where_to[None, :] == jnp.arange(GROUP)[:, None])
    pad = [(0, GROUP - slots)]
    meta = jnp.stack([
        jnp.argmax(match, axis=1).astype(jnp.int32),
        jnp.any(match, axis=1).astype(jnp.int32),
        jnp.pad(where_to.astype(jnp.int32), pad),
        jnp.pad(live.astype(jnp.int32), pad),
    ])

    def coefficients(vectors):
        return lax.dot_general(vectors, cluster_basis, contract_first, precision=high)

    def image_of(vectors, far_t):
        near = jnp.dot(near_block, vectors, precision=high)
        far = lax.dot_general(cluster_basis, far_t, contract_last, precision=high)
        return diag_shift[:, None] * vectors + (near + far)

    def gram(x, y):
        return lax.dot_general(x, y, contract_first, precision=highest)

    far_b = far_exchange(n, meta, coefficients(right_sides), couplings)
    image = image_of(right_sides, far_b)
    local = jnp.concatenate([
        gram(right_sides, right_sides), gram(right_sides, image), gram(image, image)])
    far_w, alpha, beta, updated = far_exchange(n, meta, coefficients(image), couplings, local)
    residual = right_sides - jnp.dot(image, alpha, precision=highest)
    direction = residual + jnp.dot(right_sides, beta, precision=highest)
    far_d = far_b + (gram(beta, far_b) - gram(alpha, far_w))
    image2 = image_of(direction, far_d)
    curvature = sum_all(n, gram(direction, image2), 2)
    alpha2 = local_call(second_kernel, square, "second_step", curvature, updated)
    answer = jnp.dot(right_sides, alpha, precision=highest) + jnp.dot(direction, alpha2, precision=highest)
    residual = residual - jnp.dot(image2, alpha2, precision=highest)
    return answer, residual


def solution(mesh):
    n = mesh.shape["clu"]
    in_specs = (
        P("clu", None),
        P("clu"),
        P("clu", None),
        P("clu", None),
        P("clu", None, None),
        P("clu", None),
        P("clu"),
    )
    out_specs = (P("clu", None), P("clu", None))
    return jax.shard_map(
        functools.partial(per_device, n), mesh=mesh, in_specs=in_specs,
        out_specs=out_specs, check_vma=False)
```
